128 devices in a mesh: dp: 8 (over y, core), vocab: 16 (over z, x).
Axes of the slice: x: 4, y: 4, z: 4, core: 2. Of those that a mesh axis runs over, the one named last changes fastest.
Arguments:
- pol_hidden: bfloat16 [512, 4096], P('dp'), may hold values from -16 to 16
- ref_hidden: bfloat16 [512, 4096], P('dp'), may hold values from -16 to 16
- pol_head: bfloat16 [4096, 81920], P(None, ('dp', 'vocab')), may hold values from -1 to 1
- ref_head: bfloat16 [4096, 81920], P(None, ('dp', 'vocab')), may hold values from -1 to 1
- kept: int32 [512], P('dp'), may hold values from 0 to 1, as said below
- send_counts: int32 [8, 8], P('dp'), may hold values from 0 to 32, as said below
- lengths: int32 [16], P('dp'), may hold values from 16 to 96, as said below
Outputs:
- divergences: float32 [3, 256], P(None, 'dp')
- hidden_grads: float32 [512, 4096], P(('dp', 'vocab'))
The draws below stay inside these ranges and needn't reach their ends.
Inputs may be any that keep to these rules, and one draw needn't show every extreme that they name: `kept`: 0 or 1; the number of ones among the rows of group i equals the sum of send_counts row i, and some group keeps all of its rows. `send_counts`: every column sums to exactly 32; row i sums to the kept rows of group i; some entry equals 32. `lengths`: each sequence's length is at least its kept rows plus 32 // 2.
All inputs are finite; a program needn't handle non-finite values.
Results may differ from the reference program's by a relative error of at most 0.0065.
Values may be sent and summed in bfloat16 or wider, within the bound.
A program may use at most 128 MiB of HBM per device.

```python
import jax
import jax.numpy as jnp
from jax import lax

D = 4096
VOCAB = 81920
ROWS = 64
SPAN = 32
RECV = 32
KEPT = 256
ROWS_ALL = 512
N_DP = 8


def routing_draw(key):
    key = jax.random.fold_in(key, 7)
    keys = jax.random.split(key, 4)
    half_count = N_DP // 2
    spread_draw = jax.random.randint(keys[0], (half_count,), 0, RECV + 1).at[0].set(RECV)
    loads = jnp.concatenate([RECV + spread_draw, RECV - spread_draw])
    loads = loads[jax.random.permutation(keys[1], N_DP)]
    shuffles = jax.vmap(lambda sub_key: jax.random.permutation(sub_key, ROWS))(jax.random.split(keys[2], N_DP))
    kept_grid = (shuffles < loads[:, None]).astype(jnp.int32)
    begins = jnp.cumsum(loads) - loads
    block_low = jnp.arange(N_DP) * RECV
    intersection = jnp.maximum(jnp.minimum(begins[:, None] + loads[:, None], block_low[None, :] + RECV) - jnp.maximum(begins[:, None], block_low[None, :]), 0)
    receivers = jax.random.permutation(keys[3], N_DP)
    counts = jnp.zeros((N_DP, N_DP), jnp.int32).at[:, receivers].set(intersection.astype(jnp.int32))
    return (kept_grid.reshape(-1).astype(jnp.int32), counts)


def head_pair(key):
    key = jax.random.fold_in(key, 21)
    keys = jax.random.split(key, 2)
    scale_head = 3.0 / D ** 0.5
    base_head = jnp.clip(jax.random.normal(keys[0], (D, VOCAB), jnp.float32), -6.0, 6.0)
    other_head = 0.8 * base_head + 0.6 * jnp.clip(jax.random.normal(keys[1], (D, VOCAB), jnp.float32), -6.0, 6.0)
    return (base_head * scale_head, other_head * scale_head)


def hidden_pair(key):
    inner = jax.random.fold_in(key, 31)
    keys = jax.random.split(inner, 2)
    own_part = jnp.clip(jax.random.normal(keys[0], (ROWS_ALL, D), jnp.float32), -6.0, 6.0)
    extra_part = jnp.clip(jax.random.normal(keys[1], (ROWS_ALL, D), jnp.float32), -6.0, 6.0)
    policy = own_part
    refer = 0.8 * own_part + 0.6 * extra_part
    return (policy, refer)


def draw_pol_hidden(key, part):
    return hidden_pair(key)[0].astype(jnp.bfloat16)


def draw_ref_hidden(key, part):
    return hidden_pair(key)[1].astype(jnp.bfloat16)


def draw_pol_head(key, part):
    return head_pair(key)[0].astype(jnp.bfloat16)


def draw_ref_head(key, part):
    return head_pair(key)[1].astype(jnp.bfloat16)


def draw_kept(key, part):
    return routing_draw(key)[0]


def draw_send_counts(key, part):
    return routing_draw(key)[1]


def draw_lengths(key, part):
    kept_rows = routing_draw(key)[0]
    key = jax.random.fold_in(key, 5)
    window_kept = jnp.sum(kept_rows.reshape(-1, SPAN), axis=1).astype(jnp.int32)
    extra_length = jax.random.randint(key, (ROWS_ALL // SPAN,), SPAN // 2, 2 * SPAN + 1)
    result = (window_kept + extra_length).astype(jnp.int32)
    places = jnp.arange(ROWS_ALL // SPAN, dtype=jnp.int32)
    fullest = jnp.argmax(window_kept).astype(jnp.int32)
    emptiest = jnp.argmax((window_kept == 0).astype(jnp.int32)).astype(jnp.int32)
    result = jnp.where(places == fullest, 3 * SPAN, result)
    result = jnp.where((places == emptiest) & (window_kept == 0), SPAN // 2, result)
    return result.astype(jnp.int32)


def setup_inputs(seed: int = 0) -> dict:
    key_list = jax.random.split(jax.random.key(seed), 8)
    pol_hidden = draw_pol_hidden(jax.random.fold_in(key_list[7], 71), 0)
    ref_hidden = draw_ref_hidden(jax.random.fold_in(key_list[7], 71), 0)
    pol_head = draw_pol_head(jax.random.fold_in(key_list[7], 71), 0)
    ref_head = draw_ref_head(jax.random.fold_in(key_list[7], 71), 0)
    kept = draw_kept(jax.random.fold_in(key_list[7], 71), 0)
    send_counts = draw_send_counts(jax.random.fold_in(key_list[7], 71), 0)
    lengths = draw_lengths(jax.random.fold_in(key_list[7], 71), 0)
    return {"pol_hidden": pol_hidden, "ref_hidden": ref_hidden, "pol_head": pol_head, "ref_head": ref_head, "kept": kept, "send_counts": send_counts, "lengths": lengths}


def routing(kept_all, count_all, receive):
    groups = count_all.shape[0]
    per_group = kept_all.shape[0] // groups
    kept_grid = kept_all.reshape(groups, per_group).astype(jnp.int32)
    kept_rank = (jnp.cumsum(kept_grid, axis=1) - kept_grid).astype(jnp.int32)
    starts = (jnp.cumsum(count_all, axis=1) - count_all).astype(jnp.int32)
    offsets = (jnp.cumsum(count_all, axis=0) - count_all).astype(jnp.int32)
    inside = (starts[:, None, :] <= kept_rank[:, :, None]) & (kept_rank[:, :, None] < starts[:, None, :] + count_all[:, None, :])
    target = (jnp.arange(groups, dtype=jnp.int32)[None, None, :] * receive + offsets[:, None, :] + kept_rank[:, :, None] - starts[:, None, :]).astype(jnp.int32)
    placed = jnp.sum(jnp.where(inside, target, 0), axis=2).astype(jnp.int32)
    placed = jnp.where(kept_grid > 0, placed, groups * receive).astype(jnp.int32).reshape(-1)
    anchor = jnp.zeros((groups * receive,), jnp.int32).at[placed].set(jnp.arange(groups * per_group, dtype=jnp.int32), mode="drop")
    return placed, anchor


def row_weights(kept_all, length_all, seq_span):
    repeated = jnp.repeat(length_all, seq_span).astype(jnp.float32)
    return kept_all.astype(jnp.float32) * (jnp.float32(seq_span) / repeated)


def head_terms(pol_rows, ref_rows, weight_rows, pol_head, ref_head):
    pol_logits = jnp.dot(pol_rows, pol_head, preferred_element_type=jnp.float32)
    ref_logits = jnp.dot(ref_rows, ref_head, preferred_element_type=jnp.float32)
    pol_log = pol_logits - jax.nn.logsumexp(pol_logits, axis=1, keepdims=True)
    ref_log = ref_logits - jax.nn.logsumexp(ref_logits, axis=1, keepdims=True)
    differ = pol_log - ref_log
    pol_prob = jnp.exp(pol_log)
    ref_prob = jnp.exp(ref_log)
    forward_kl = jnp.sum(pol_prob * differ, axis=1)
    squared_kl = 0.5 * jnp.sum(pol_prob * differ * differ, axis=1)
    reverse_kl = -jnp.sum(ref_prob * differ, axis=1)
    slope_rows = (weight_rows[:, None] * pol_prob * (0.5 * differ * differ + differ - (forward_kl + squared_kl)[:, None])).astype(jnp.bfloat16)
    back_rows = lax.dot_general(slope_rows, pol_head, (((1,), (1,)), ((), ())), preferred_element_type=jnp.float32)
    return jnp.stack([forward_kl, squared_kl, reverse_kl]), back_rows


def reference(pol_hidden, ref_hidden, pol_head, ref_head, kept, send_counts, lengths):
    placed, anchor = routing(kept, send_counts, RECV)
    weights = row_weights(kept, lengths, SPAN)[anchor]
    pol_rows = pol_hidden[anchor].reshape(N_DP, RECV, D)
    ref_rows = ref_hidden[anchor].reshape(N_DP, RECV, D)

    def one_block(block_items):
        return head_terms(block_items[0], block_items[1], block_items[2], pol_head, ref_head)

    block_divs, block_grads = lax.map(one_block, (pol_rows, ref_rows, weights.reshape(N_DP, RECV)))
    divergences = jnp.transpose(block_divs, (1, 0, 2)).reshape(3, KEPT)
    hidden_grads = jnp.zeros((ROWS_ALL, D), jnp.float32).at[anchor].set(block_grads.reshape(KEPT, D))
    return divergences, hidden_grads
```

```python
import functools

import jax
import jax.numpy as jnp
from jax import lax
from jax.experimental import pallas as pl
from jax.experimental.pallas import tpu as pltpu
from jax.sharding import PartitionSpec as P

MESH = pl.DeviceIdType.MESH
GROUPS = 8
PEERS = 16
SPAN = 32
F32 = jnp.float32
BF16 = jnp.bfloat16


def dot(a, b):
    return lax.dot_general(a, b, (((1,), (0,)), ((), ())), preferred_element_type=F32)


def dot_t(a, b):
    return lax.dot_general(a, b, (((1,), (1,)), ((), ())), preferred_element_type=F32)


def iota(shape, axis):
    return lax.broadcasted_iota(jnp.int32, shape, axis)


def merge_stats(block):
    top_p, top_r = block[:, 0, :], block[:, 1, :]
    s0, s1, s2 = block[:, 2, :], block[:, 3, :], block[:, 4, :]
    r0, r1 = block[:, 5, :], block[:, 6, :]
    best_p = jnp.max(top_p, axis=0, keepdims=True)
    best_r = jnp.max(top_r, axis=0, keepdims=True)
    low_p, low_r = top_p - best_p, top_r - best_r
    shift = low_p - low_r
    scale_p, scale_r = jnp.exp(low_p), jnp.exp(low_r)

    def total(value):
        return jnp.sum(value, axis=0, keepdims=True)

    return (
        best_p,
        best_r,
        total(scale_p * s0),
        total(scale_p * (s1 + shift * s0)),
        total(scale_p * (s2 + shift * (2.0 * s1 + shift * s0))),
        total(scale_r * r0),
        total(scale_r * (r1 + shift * r0)),
    )


def kernel(
    pol_hidden,
    ref_hidden,
    pol_head,
    ref_head,
    kept,
    counts,
    lengths,
    div_out,
    grad_out,
    head,
    gath,
    rows,
    acc,
    logt,
    slope,
    info,
    sel,
    selt,
    length_row,
    stat_v,
    stat_d,
    a_src,
    a_dst,
    own,
    b1_src,
    b1_half,
    b1_full,
    b2_src,
    b2_half,
    b2_full,
    c_src,
    c_dst,
    d_src,
    d_dst,
    head_sem,
    local_sem,
    p1_send,
    p1_recv,
    info_send,
    info_recv,
    ring_send,
    ring_recv,
    sib_send,
    sib_recv,
    sv_send,
    sv_recv,
    sd_send,
    sd_recv,
    a_send,
    a_recv,
    b1_send,
    b1_recv,
    b2_send,
    b2_recv,
    c_send,
    c_recv,
    d_send,
    d_recv,
):
    group = lax.axis_index("dp")
    v = lax.axis_index("vocab")
    y, c = group // 2, group % 2
    z, x = v // 4, v % 4
    f = x * (1 - c) + z * c
    s = z * (1 - c) + x * c
    per_group, width = pol_hidden.shape
    part = width // PEERS
    half = width // 2
    shard = pol_head.shape[1]
    n_rows = rows.shape[2]
    mid = n_rows // 2

    def vid(df, ds):
        ff, ss = (f + df) % 4, (s + ds) % 4
        return ff * (1 + 3 * c) + ss * (4 - 3 * c)

    def remote(src, dst, send, recv, dp=None, vocab=None):
        target = {}
        if dp is not None:
            target["dp"] = dp
        if vocab is not None:
            target["vocab"] = vocab
        return pltpu.make_async_remote_copy(
            src_ref=src,
            dst_ref=dst,
            send_sem=send,
            recv_sem=recv,
            device_id=target,
            device_id_type=MESH,
        )

    sibling = group + 1 - 2 * c

    head_copies = []
    quarter = width // 4
    for m, source in enumerate((pol_head, ref_head)):
        for q in range(4):
            at = pl.ds(q * quarter, quarter)
            copy = pltpu.make_async_copy(source.at[at], head.at[m, at], head_sem.at[m, q])
            copy.start()
            head_copies.append(copy)
    barrier = pltpu.get_barrier_semaphore()
    for j in range(1, GROUPS):
        pl.semaphore_signal(
            barrier, inc=1, device_id={"dp": (group + j) % GROUPS}, device_id_type=MESH
        )
    for j in range(1, PEERS):
        pl.semaphore_signal(
            barrier, inc=1, device_id={"vocab": (v + j) % PEERS}, device_id_type=MESH
        )
    info[group] = jnp.zeros(info.shape[1:], jnp.int32)
    info[group, 0:1, 0:per_group] = kept[...]
    info[group, 1:2, 0:GROUPS] = counts[...]
    info[group, 2:3, 0:2] = lengths[...]
    pl.semaphore_wait(barrier, GROUPS + PEERS - 2)

    columns = pl.ds(pl.multiple_of(v * part, part), part)
    for j in range(1, GROUPS):
        remote(
            info.at[group],
            info.at[group],
            info_send.at[j],
            info_recv.at[group],
            dp=(group + j) % GROUPS,
        ).start()
    hiddens = (pol_hidden, ref_hidden)

    def part_copy(m, dy):
        return remote(
            hiddens[m].at[:, columns],
            gath.at[group],
            p1_send.at[dy, m],
            p1_recv.at[group],
            dp=2 * ((y + dy) % 4) + m,
        )

    for dy in (2, 1, 3):
        for m in (0, 1):
            part_copy(m, dy).start()

    def local_copy(m):
        return pltpu.make_async_copy(hiddens[m].at[:, columns], gath.at[group], local_sem.at[0])

    for m in (0, 1):

        @pl.when(c == m)
        def _():
            local_copy(m).start()

        @pl.when(c != m)
        def _():
            part_copy(m, 0).start()

    acc[...] = jnp.zeros(acc.shape, F32)

    for j in range(1, GROUPS):
        other = (group + j) % GROUPS
        remote(
            info.at[other], info.at[other], info_send.at[j], info_recv.at[other], dp=other
        ).wait_recv()
    kept_g = jnp.concatenate([info[i, 0:1, :] for i in range(GROUPS)], axis=0).astype(F32)
    count_g = jnp.concatenate([info[i, 1:2, :] for i in range(GROUPS)], axis=0).astype(F32)
    length_g = jnp.concatenate([info[i, 2:3, :] for i in range(GROUPS)], axis=0).astype(F32)
    upper = (iota((128, 128), 0) < iota((128, 128), 1)).astype(F32)
    rank = dot(kept_g, upper)
    start = dot(count_g, upper)
    line = jnp.zeros((1, 128), F32)
    lines = []
    for i in range(GROUPS):
        lines.append(line)
        line = line + count_g[i : i + 1, :]
    offset = jnp.concatenate(lines, axis=0)
    placed = jnp.zeros((GROUPS, 128), F32)
    for j in range(GROUPS):
        first = start[:, j : j + 1]
        last = first + count_g[:, j : j + 1]
        target = float(j * (n_rows // GROUPS)) + offset[:, j : j + 1] + rank - first
        placed = placed + jnp.where((first <= rank) & (rank < last), target, 0.0)
    placed = jnp.where(kept_g > 0.5, placed, -1.0)
    lane = iota((GROUPS, 128), 1)
    length_g = jnp.where(lane < SPAN, length_g[:, 0:1], length_g[:, 1:2])
    length_g = jnp.where(kept_g > 0.5, length_g, 0.0)
    placed_r = pltpu.roll(placed, 64, 1)
    length_r = pltpu.roll(length_g, 64, 1)
    place = iota((n_rows, 128), 0).astype(F32)
    low = lane[0:1] < 64
    weight_len = jnp.zeros((8, n_rows), F32)
    for k in range(4):
        pair = jnp.where(low, placed[2 * k : 2 * k + 1], placed_r[2 * k + 1 : 2 * k + 2])
        spans = jnp.where(low, length_g[2 * k : 2 * k + 1], length_r[2 * k + 1 : 2 * k + 2])
        chosen = (place == pair).astype(F32)
        sel[:, k * 128 : (k + 1) * 128] = chosen.astype(BF16)
        weight_len = weight_len + dot_t(jnp.broadcast_to(spans, (8, 128)), chosen)
    length_row[...] = weight_len

    for j in range(1, GROUPS):
        other = (group + j) % GROUPS
        remote(
            gath.at[other], gath.at[other], p1_send.at[0, 0], p1_recv.at[other], dp=other
        ).wait_recv()
    local_copy(0).wait()
    rows[c, v] = dot(sel[...], gath[...].reshape(GROUPS * per_group, part)).astype(BF16)

    upper_half, lower_half = pl.ds(0, mid), pl.ds(mid, mid)

    def block(slot, cut=None):
        return rows.at[c, slot] if cut is None else rows.at[c, slot, cut]

    def push(slot, index, target, cut=None, sem=0):
        remote(
            block(slot, cut),
            block(slot, cut),
            ring_send.at[index],
            ring_recv.at[slot, sem],
            vocab=target,
        ).start()

    def arrive(slot, cut=None, sem=0):
        remote(
            block(slot, cut),
            block(slot, cut),
            ring_send.at[0],
            ring_recv.at[slot, sem],
            vocab=vid(1, 0),
        ).wait_recv()

    def share(slot):
        remote(
            block(slot), block(slot), sib_send.at[slot], sib_recv.at[slot], dp=sibling
        ).start()

    f_up, f_down, s_up, s_down = vid(1, 0), vid(-1, 0), vid(0, 1), vid(0, -1)

    def multiply(model, slot):
        at = pl.ds(pl.multiple_of(slot * part, part), part)
        acc[model] += dot(rows[model, slot], head[model, at, :])

    def multiply_sibling(slot):
        remote(
            rows.at[1 - c, slot],
            rows.at[1 - c, slot],
            sib_send.at[slot],
            sib_recv.at[slot],
            dp=sibling,
        ).wait_recv()

    push(v, 0, f_up)
    push(v, 1, f_down)
    push(v, 4, s_up)
    push(v, 5, s_down)
    share(v)
    selt[...] = jnp.transpose(sel[...].astype(F32)).astype(BF16)
    for copy in head_copies:
        copy.wait()

    slot = vid(-1, 0)
    arrive(slot)
    push(slot, 2, f_up, upper_half, 0)
    push(slot, 6, s_up)
    push(slot, 7, s_down)
    share(slot)
    slot = vid(1, 0)
    arrive(slot)
    push(slot, 3, f_down, lower_half, 1)
    push(slot, 8, s_up)
    push(slot, 9, s_down)
    share(slot)
    slot = vid(2, 0)
    arrive(slot, upper_half, 0)
    arrive(slot, lower_half, 1)
    push(slot, 10, s_up)
    push(slot, 11, s_down)
    share(slot)

    def order(b):
        return jnp.where(b == 1, 3, jnp.where(b == 2, 1, jnp.where(b == 3, 2, 0)))

    def first_multiply(i, carry):
        df = order(i // 2)

        @pl.when(i % 2 == 1)
        def _():
            multiply_sibling(vid(0, df))

        multiply(
            jnp.where(i % 2 == 0, c, 1 - c), jnp.where(i % 2 == 0, vid(df, 0), vid(0, df))
        )
        return carry

    def second(b, carry):
        df = order(b)
        low_slot, high_slot = vid(df, -1), vid(df, 1)
        arrive(low_slot)
        push(low_slot, 12 + b, s_up, upper_half, 0)
        share(low_slot)
        arrive(high_slot)
        push(high_slot, 16 + b, s_down, lower_half, 1)
        share(high_slot)

        def inner(i, carry):
            ds = jnp.where(i % 2 == 0, -1, 1)
            mine = i < 2

            @pl.when(i >= 2)
            def _():
                multiply_sibling(vid(ds, df))

            multiply(jnp.where(mine, c, 1 - c), jnp.where(mine, vid(df, ds), vid(ds, df)))
            return carry

        lax.fori_loop(0, 4, inner, 0)
        return carry

    def third(b, carry):
        df = order(b)
        slot = vid(df, 2)
        arrive(slot, upper_half, 0)
        arrive(slot, lower_half, 1)
        share(slot)

        def inner(i, carry):
            @pl.when(i == 1)
            def _():
                multiply_sibling(vid(2, df))

            multiply(jnp.where(i == 0, c, 1 - c), jnp.where(i == 0, vid(df, 2), vid(2, df)))
            return carry

        lax.fori_loop(0, 2, inner, 0)
        return carry

    lax.fori_loop(0, 8, first_multiply, 0)
    lax.fori_loop(0, 4, second, 0)
    lax.fori_loop(0, 4, third, 0)

    chunks = shard // 128
    for m in (0, 1):
        for q in range(chunks):
            at = slice(q * 128, (q + 1) * 128)
            logt[m, at, :] = jnp.transpose(acc[m, :, at])
    top_p = jnp.max(logt[0], axis=0, keepdims=True)
    top_r = jnp.max(logt[1], axis=0, keepdims=True)
    step = 32
    zero = jnp.zeros((8, n_rows), F32)

    def fold(value):
        return jnp.sum(value.reshape(step // 8, 8, n_rows), axis=0)

    def local_sums(q, carry):
        s0, s1, s2, r0, r1 = carry
        at = pl.ds(pl.multiple_of(q * step, step), step)
        lp = logt[0, at, :] - top_p
        lr = logt[1, at, :] - top_r
        ep, er = jnp.exp(lp), jnp.exp(lr)
        d = lp - lr
        ed = ep * d
        return (
            s0 + fold(ep),
            s1 + fold(ed),
            s2 + fold(ed * d),
            r0 + fold(er),
            r1 + fold(er * d),
        )

    sums = lax.fori_loop(0, shard // step, local_sums, (zero,) * 5)
    sums = [jnp.sum(value, axis=0, keepdims=True) for value in sums]
    blank = jnp.zeros((1, n_rows), F32)
    stat_v[v] = jnp.concatenate([top_p, top_r, *sums, blank], axis=0)
    for j in range(1, PEERS):
        remote(
            stat_v.at[v], stat_v.at[v], sv_send.at[j], sv_recv.at[v], vocab=(v + j) % PEERS
        ).start()
    for j in range(1, PEERS):
        other = (v + j) % PEERS
        remote(
            stat_v.at[other], stat_v.at[other], sv_send.at[j], sv_recv.at[other], vocab=other
        ).wait_recv()
    stat_d[group] = jnp.concatenate([*merge_stats(stat_v), blank], axis=0)
    for j in range(1, GROUPS):
        remote(
            stat_d.at[group],
            stat_d.at[group],
            sd_send.at[j],
            sd_recv.at[group],
            dp=(group + j) % GROUPS,
        ).start()
    for j in range(1, GROUPS):
        other = (group + j) % GROUPS
        remote(
            stat_d.at[other], stat_d.at[other], sd_send.at[j], sd_recv.at[other], dp=other
        ).wait_recv()
    top_p, top_r, s0, s1, s2, r0, r1 = merge_stats(stat_d)
    log_s, log_r = jnp.log(s0), jnp.log(r0)
    norm_p, norm_r = top_p + log_s, top_r + log_r
    move = log_r - log_s
    forward = s1 / s0 + move
    squared = 0.5 * ((s2 + move * (2.0 * s1)) / s0 + move * move)
    reverse = -(r1 / r0 + move)
    both = forward + squared
    weight = float(SPAN) / length_row[0:1, :]

    def slopes(q, carry):
        at = pl.ds(pl.multiple_of(q * step, step), step)
        lp = logt[0, at, :] - norm_p
        d = lp - (logt[1, at, :] - norm_r)
        slope[at, :] = (weight * jnp.exp(lp) * (0.5 * d * d + d - both)).astype(BF16)
        return carry

    lax.fori_loop(0, shard // step, slopes, 0)

    chunk = half // 4
    order_s = (2, 1, 3, 0)

    def start_of(core, index):
        return pl.multiple_of(core * half + index * chunk, chunk)

    def a_copy(t):
        return remote(a_src.at[t], a_dst.at[t], a_send.at[t], a_recv.at[t], dp=sibling)

    for t in range(4):
        theirs = start_of(1 - c, (f + order_s[t]) % 4)
        a_src[t] = dot(head[0, pl.ds(theirs, chunk), :], slope[...]).astype(BF16)
        a_copy(t).start()
        mine = start_of(c, (s + order_s[t]) % 4)
        own[t] = dot(head[0, pl.ds(mine, chunk), :], slope[...])

    hc = chunk // 2

    def b1_copy(index):
        if index < 2:
            return remote(
                b1_src.at[0, pl.ds(index * hc, hc)],
                b1_half.at[index],
                b1_send.at[index],
                b1_recv.at[index],
                vocab=(s_up, s_down)[index],
            )
        return remote(
            b1_src.at[index - 1],
            b1_full.at[index - 2],
            b1_send.at[index],
            b1_recv.at[index],
            vocab=(s_up, s_down)[index - 2],
        )

    a_copy(0).wait_recv()
    b1_src[0] = (own[0] + a_dst[0].astype(F32)).astype(BF16)
    b1_copy(0).start()
    b1_copy(1).start()
    a_copy(1).wait_recv()
    own[1] = own[1] + a_dst[1].astype(F32)
    a_copy(2).wait_recv()
    own[2] = own[2] + a_dst[2].astype(F32)
    b1_copy(0).wait_recv()
    b1_src[1, 0:hc] = (own[1, 0:hc] + b1_half[0].astype(F32)).astype(BF16)
    b1_src[1, hc:chunk] = own[1, hc:chunk].astype(BF16)
    b1_copy(2).start()
    b1_copy(1).wait_recv()
    b1_src[2, 0:hc] = own[2, 0:hc].astype(BF16)
    b1_src[2, hc:chunk] = (own[2, hc:chunk] + b1_half[1].astype(F32)).astype(BF16)
    b1_copy(3).start()
    a_copy(3).wait_recv()
    own[3] = own[3] + a_dst[3].astype(F32)
    b1_copy(2).wait_recv()
    b1_copy(3).wait_recv()
    own[3] = own[3] + b1_full[0].astype(F32) + b1_full[1].astype(F32)

    piece = chunk // 4
    hp = piece // 2

    def b2_copy(index):
        if index < 2:
            return remote(
                b2_src.at[0, pl.ds(index * hp, hp)],
                b2_half.at[index],
                b2_send.at[index],
                b2_recv.at[index],
                vocab=(f_up, f_down)[index],
            )
        return remote(
            b2_src.at[index - 1],
            b2_full.at[index - 2],
            b2_send.at[index],
            b2_recv.at[index],
            vocab=(f_up, f_down)[index - 2],
        )

    def sum_at(df, begin, count):
        at = pl.multiple_of(((f + df) % 4) * piece + begin, count)
        return own[3, pl.ds(at, count), :]

    b2_src[0] = sum_at(2, 0, piece).astype(BF16)
    b2_copy(0).start()
    b2_copy(1).start()
    b2_copy(0).wait_recv()
    b2_src[1, 0:hp] = (sum_at(1, 0, hp) + b2_half[0].astype(F32)).astype(BF16)
    b2_src[1, hp:piece] = sum_at(1, hp, hp).astype(BF16)
    b2_copy(2).start()
    b2_copy(1).wait_recv()
    b2_src[2, 0:hp] = sum_at(-1, 0, hp).astype(BF16)
    b2_src[2, hp:piece] = (sum_at(-1, hp, hp) + b2_half[1].astype(F32)).astype(BF16)
    b2_copy(3).start()
    b2_copy(2).wait_recv()
    b2_copy(3).wait_recv()
    total = sum_at(0, 0, piece) + b2_full[0].astype(F32) + b2_full[1].astype(F32)

    spread = dot_t(selt[...], total.astype(BF16)).astype(BF16)
    c_src[...] = spread.reshape(GROUPS, per_group, piece)
    for j in range(1, GROUPS):
        other = (group + j) % GROUPS
        remote(
            c_src.at[other], c_dst.at[group], c_send.at[j], c_recv.at[group], dp=other
        ).start()
    c_dst[group] = c_src[group]

    stacked = jnp.concatenate([forward, squared, reverse], axis=0)
    share_rows = n_rows // GROUPS
    result = jnp.zeros((3, share_rows), F32)
    for j in range(GROUPS):
        result = jnp.where(group == j, stacked[:, j * share_rows : (j + 1) * share_rows], result)
    div_out[...] = result

    for j in range(1, GROUPS):
        other = (group + j) % GROUPS
        remote(
            c_src.at[other], c_dst.at[other], c_send.at[j], c_recv.at[other], dp=other
        ).wait_recv()
    for core in (0, 1):
        value = c_dst[core].astype(F32)
        for k in range(1, 4):
            value = value + c_dst[2 * k + core].astype(F32)
        d_src[:, core * piece : (core + 1) * piece] = value

    def eight(index):
        return pl.ds(pl.multiple_of(8 * (index // 2), 8), 8)

    for j in range(1, PEERS):
        other = (v + j) % PEERS
        remote(
            d_src.at[eight(other)], d_dst.at[v], d_send.at[j], d_recv.at[v], vocab=other
        ).start()
    d_dst[v] = d_src[eight(v), :]
    for j in range(1, PEERS):
        other = (v + j) % PEERS
        remote(
            d_src.at[eight(other)], d_dst.at[other], d_send.at[j], d_recv.at[other], vocab=other
        ).wait_recv()
    odd = v % 2 == 1
    for u in range(PEERS):
        picked = jnp.where(odd, d_dst[u, 4:8, :], d_dst[u, 0:4, :])
        at0 = u * piece
        at1 = half + ((u % 4) * 4 + u // 4) * piece
        grad_out[:, at0 : at0 + piece] = picked[:, 0:piece]
        grad_out[:, at1 : at1 + piece] = picked[:, piece : 2 * piece]

    for j in range(1, GROUPS):
        other = (group + j) % GROUPS
        remote(
            info.at[group], info.at[group], info_send.at[j], info_recv.at[group], dp=other
        ).wait_send()
        remote(
            stat_d.at[group], stat_d.at[group], sd_send.at[j], sd_recv.at[group], dp=other
        ).wait_send()
        remote(
            c_src.at[other], c_dst.at[group], c_send.at[j], c_recv.at[group], dp=other
        ).wait_send()
    for dy in (1, 2, 3):
        for m in (0, 1):
            part_copy(m, dy).wait_send()
    for m in (0, 1):

        @pl.when(c != m)
        def _():
            part_copy(m, 0).wait_send()

    for j in range(1, PEERS):
        other = (v + j) % PEERS
        remote(
            stat_v.at[v], stat_v.at[v], sv_send.at[j], sv_recv.at[v], vocab=other
        ).wait_send()
        remote(
            d_src.at[eight(other)], d_dst.at[v], d_send.at[j], d_recv.at[v], vocab=other
        ).wait_send()

    def sent(index, cut=None):
        remote(
            block(v, cut), block(v, cut), ring_send.at[index], ring_recv.at[v, 0], vocab=f_up
        ).wait_send()

    for index in (0, 1, *range(4, 12)):
        sent(index)
    for index in (2, 3, *range(12, 20)):
        sent(index, upper_half)
    for slot in range(PEERS):
        remote(
            block(slot), block(slot), sib_send.at[slot], sib_recv.at[slot], dp=sibling
        ).wait_send()
    for t in range(4):
        a_copy(t).wait_send()
        b1_copy(t).wait_send()
        b2_copy(t).wait_send()


def body(pol_hidden, ref_hidden, pol_head, ref_head, kept, send_counts, lengths):
    per_group, width = pol_hidden.shape
    shard = pol_head.shape[1]
    n_rows = GROUPS * per_group // 2
    part = width // PEERS
    chunk = width // 8
    piece = chunk // 4
    vmem = pl.BlockSpec(memory_space=pltpu.VMEM)
    hbm = pl.BlockSpec(memory_space=pl.ANY)
    dma = pltpu.SemaphoreType.DMA
    return pl.pallas_call(
        kernel,
        out_shape=(
            jax.ShapeDtypeStruct((3, n_rows // GROUPS), F32),
            jax.ShapeDtypeStruct((4, width), F32),
        ),
        in_specs=[hbm, hbm, hbm, hbm, vmem, vmem, vmem],
        out_specs=(vmem, vmem),
        scratch_shapes=[
            pltpu.VMEM((2, width, shard), BF16),
            pltpu.VMEM((GROUPS, per_group, part), BF16),
            pltpu.VMEM((2, PEERS, n_rows, part), BF16),
            pltpu.VMEM((2, n_rows, shard), F32),
            pltpu.VMEM((2, shard, n_rows), F32),
            pltpu.VMEM((shard, n_rows), BF16),
            pltpu.VMEM((GROUPS, 8, 128), jnp.int32),
            pltpu.VMEM((n_rows, 2 * n_rows), BF16),
            pltpu.VMEM((2 * n_rows, n_rows), BF16),
            pltpu.VMEM((8, n_rows), F32),
            pltpu.VMEM((PEERS, 8, n_rows), F32),
            pltpu.VMEM((GROUPS, 8, n_rows), F32),
            pltpu.VMEM((4, chunk, n_rows), BF16),
            pltpu.VMEM((4, chunk, n_rows), BF16),
            pltpu.VMEM((4, chunk, n_rows), F32),
            pltpu.VMEM((3, chunk, n_rows), BF16),
            pltpu.VMEM((2, chunk // 2, n_rows), BF16),
            pltpu.VMEM((2, chunk, n_rows), BF16),
            pltpu.VMEM((3, piece, n_rows), BF16),
            pltpu.VMEM((2, piece // 2, n_rows), BF16),
            pltpu.VMEM((2, piece, n_rows), BF16),
            pltpu.VMEM((GROUPS, per_group, piece), BF16),
            pltpu.VMEM((GROUPS, per_group, piece), BF16),
            pltpu.VMEM((per_group, 2 * piece), F32),
            pltpu.VMEM((PEERS, 8, 2 * piece), F32),
            dma((2, 4)),
            dma((1,)),
            dma((4, 2)),
            dma((GROUPS,)),
            dma((GROUPS,)),
            dma((GROUPS,)),
            dma((20,)),
            dma((PEERS, 2)),
            dma((PEERS,)),
            dma((PEERS,)),
            dma((PEERS,)),
            dma((PEERS,)),
            dma((GROUPS,)),
            dma((GROUPS,)),
            dma((4,)),
            dma((4,)),
            dma((4,)),
            dma((4,)),
            dma((4,)),
            dma((4,)),
            dma((GROUPS,)),
            dma((GROUPS,)),
            dma((PEERS,)),
            dma((PEERS,)),
        ],
        compiler_params=pltpu.CompilerParams(
            collective_id=0, has_side_effects=True, vmem_limit_bytes=56 * 1024 * 1024
        ),
        cost_estimate=pl.CostEstimate(
            flops=6 * n_rows * width * shard, bytes_accessed=4 * width * shard, transcendentals=0
        ),
        name="divergence_heads",
    )(
        pol_hidden,
        ref_hidden,
        pol_head,
        ref_head,
        kept.reshape(1, per_group),
        send_counts,
        lengths.reshape(1, 2),
    )


def solution(mesh):
    return jax.shard_map(
        body,
        mesh=mesh,
        in_specs=(
            P("dp", None),
            P("dp", None),
            P(None, ("dp", "vocab")),
            P(None, ("dp", "vocab")),
            P("dp"),
            P("dp", None),
            P("dp"),
        ),
        out_specs=(P(None, "dp"), P(("dp", "vocab"), None)),
        check_vma=False,
    )
```

```python
import functools

import jax
import jax.numpy as jnp
from jax import lax
from jax.experimental import pallas as pl
from jax.experimental.pallas import tpu as pltpu
from jax.sharding import PartitionSpec as P

MESH = pl.DeviceIdType.MESH
GROUPS = 8
PEERS = 16
SPAN = 32
LAG = 2
AHEAD = 2
F32 = jnp.float32
BF16 = jnp.bfloat16


def dot(a, b):
    return lax.dot_general(a, b, (((1,), (0,)), ((), ())), preferred_element_type=F32)


def dot_t(a, b):
    return lax.dot_general(a, b, (((1,), (1,)), ((), ())), preferred_element_type=F32)


def iota(shape, axis):
    return lax.broadcasted_iota(jnp.int32, shape, axis)


def merge_stats(block):
    top_p, top_r = block[:, 0, :], block[:, 1, :]
    s0, s1, s2 = block[:, 2, :], block[:, 3, :], block[:, 4, :]
    r0, r1 = block[:, 5, :], block[:, 6, :]
    best_p = jnp.max(top_p, axis=0, keepdims=True)
    best_r = jnp.max(top_r, axis=0, keepdims=True)
    low_p, low_r = top_p - best_p, top_r - best_r
    shift = low_p - low_r
    scale_p, scale_r = jnp.exp(low_p), jnp.exp(low_r)

    def total(value):
        return jnp.sum(value, axis=0, keepdims=True)

    return (
        best_p,
        best_r,
        total(scale_p * s0),
        total(scale_p * (s1 + shift * s0)),
        total(scale_p * (s2 + shift * (2.0 * s1 + shift * s0))),
        total(scale_r * r0),
        total(scale_r * (r1 + shift * r0)),
    )


def kernel(
    pol_hidden,
    ref_hidden,
    pol_head,
    ref_head,
    kept,
    counts,
    lengths,
    div_out,
    grad_out,
    head,
    gath,
    rows,
    acc,
    logt,
    slope,
    info,
    sel,
    selt,
    length_row,
    stat_v,
    stat_d,
    a_src,
    a_dst,
    own,
    b_src,
    b_dst,
    c_src,
    c_dst,
    d_src,
    d_dst,
    head_sem,
    local_sem,
    p1_send,
    p1_recv,
    info_send,
    info_recv,
    ring_send,
    ring_recv,
    sib_send,
    sib_recv,
    token,
    sv_send,
    sv_recv,
    sd_send,
    sd_recv,
    a_send,
    a_recv,
    b_send,
    b_recv,
    c_send,
    c_recv,
    d_send,
    d_recv,
):
    group = lax.axis_index("dp")
    v = lax.axis_index("vocab")
    y, c = group // 2, group % 2
    z, x = v // 4, v % 4
    f = x * (1 - c) + z * c
    s = z * (1 - c) + x * c
    per_group, width = pol_hidden.shape
    part = width // PEERS
    half = width // 2
    shard = pol_head.shape[1]
    n_rows = rows.shape[2]

    def vid(df, ds):
        ff, ss = (f + df) % 4, (s + ds) % 4
        return ff * (1 + 3 * c) + ss * (4 - 3 * c)

    def remote(src, dst, send, recv, dp=None, vocab=None):
        target = {}
        if dp is not None:
            target["dp"] = dp
        if vocab is not None:
            target["vocab"] = vocab
        return pltpu.make_async_remote_copy(
            src_ref=src,
            dst_ref=dst,
            send_sem=send,
            recv_sem=recv,
            device_id=target,
            device_id_type=MESH,
        )

    sibling = group + 1 - 2 * c
    drains = []

    def finish():
        for drain in drains:
            drain()


    head_copies = []
    quarter = width // 4
    for m, source in enumerate((pol_head, ref_head)):
        for q in range(4):
            at = pl.ds(q * quarter, quarter)
            copy = pltpu.make_async_copy(source.at[at], head.at[m, at], head_sem.at[m, q])
            copy.start()
            head_copies.append(copy)
    barrier = pltpu.get_barrier_semaphore()
    for j in range(1, GROUPS):
        pl.semaphore_signal(
            barrier, inc=1, device_id={"dp": (group + j) % GROUPS}, device_id_type=MESH
        )
    for ds in (1, 2, 3):
        pl.semaphore_signal(
            barrier, inc=1, device_id={"vocab": vid(0, ds)}, device_id_type=MESH
        )
    info[group] = jnp.zeros(info.shape[1:], jnp.int32)
    info[group, 0:1, 0:per_group] = kept[...]
    info[group, 1:2, 0:GROUPS] = counts[...]
    info[group, 2:3, 0:2] = lengths[...]
    pl.semaphore_wait(barrier, GROUPS + 2)

    for j in range(1, GROUPS):
        remote(
            info.at[group],
            info.at[group],
            info_send.at[j],
            info_recv.at[group],
            dp=(group + j) % GROUPS,
        ).start()
    hiddens = (pol_hidden, ref_hidden)

    def part_source(m, q):
        at = pl.multiple_of(((z, x)[m] * 4 + q) * part, part)
        return hiddens[m].at[:, pl.ds(at, part)]

    def part_copy(m, dy, q):
        return remote(
            part_source(m, q),
            gath.at[q, group],
            p1_send.at[q, 2 * dy + m],
            p1_recv.at[q, group],
            dp=2 * ((y + dy) % 4) + m,
        )

    def local_copy(m, q):
        return pltpu.make_async_copy(part_source(m, q), gath.at[q, group], local_sem.at[q])

    def each_part(q, act):
        for dy in (2, 1, 3):
            for m in (0, 1):
                act(part_copy(m, dy, q))
        for m in (0, 1):

            @pl.when(c != m)
            def _():
                act(part_copy(m, 0, q))

    def start_parts(q):
        each_part(q, lambda copy: copy.start())
        for m in (0, 1):

            @pl.when(c == m)
            def _():
                local_copy(m, q).start()

    for q in range(AHEAD):
        start_parts(q)

    acc[...] = jnp.zeros(acc.shape, F32)

    def drain_parts():
        for j in range(1, GROUPS):
            remote(
                info.at[group],
                info.at[group],
                info_send.at[j],
                info_recv.at[group],
                dp=(group + j) % GROUPS,
            ).wait_send()
        for q in range(4 - AHEAD, 4):
            each_part(q, lambda copy: copy.wait_send())

    drains.append(drain_parts)

    for j in range(1, GROUPS):
        other = (group + j) % GROUPS
        remote(
            info.at[other], info.at[other], info_send.at[j], info_recv.at[other], dp=other
        ).wait_recv()
    kept_g = jnp.concatenate([info[i, 0:1, :] for i in range(GROUPS)], axis=0).astype(F32)
    count_g = jnp.concatenate([info[i, 1:2, :] for i in range(GROUPS)], axis=0).astype(F32)
    length_g = jnp.concatenate([info[i, 2:3, :] for i in range(GROUPS)], axis=0).astype(F32)
    upper = (iota((128, 128), 0) < iota((128, 128), 1)).astype(F32)
    rank = dot(kept_g, upper)
    start = dot(count_g, upper)
    line = jnp.zeros((1, 128), F32)
    lines = []
    for i in range(GROUPS):
        lines.append(line)
        line = line + count_g[i : i + 1, :]
    offset = jnp.concatenate(lines, axis=0)
    placed = jnp.zeros((GROUPS, 128), F32)
    for j in range(GROUPS):
        first = start[:, j : j + 1]
        last = first + count_g[:, j : j + 1]
        target = float(j * (n_rows // GROUPS)) + offset[:, j : j + 1] + rank - first
        placed = placed + jnp.where((first <= rank) & (rank < last), target, 0.0)
    placed = jnp.where(kept_g > 0.5, placed, -1.0)
    lane = iota((GROUPS, 128), 1)
    length_g = jnp.where(lane < SPAN, length_g[:, 0:1], length_g[:, 1:2])
    length_g = jnp.where(kept_g > 0.5, length_g, 0.0)
    placed_r = pltpu.roll(placed, 64, 1)
    length_r = pltpu.roll(length_g, 64, 1)
    place = iota((n_rows, 128), 0).astype(F32)
    low = lane[0:1] < 64
    weight_len = jnp.zeros((8, n_rows), F32)
    for k in range(4):
        pair = jnp.where(low, placed[2 * k : 2 * k + 1], placed_r[2 * k + 1 : 2 * k + 2])
        spans = jnp.where(low, length_g[2 * k : 2 * k + 1], length_r[2 * k + 1 : 2 * k + 2])
        chosen = (place == pair).astype(F32)
        sel[:, k * 128 : (k + 1) * 128] = chosen.astype(BF16)
        weight_len = weight_len + dot_t(jnp.broadcast_to(spans, (8, 128)), chosen)
    length_row[...] = weight_len

    line = iota((2 * n_rows, 2 * n_rows), 0)
    to_f, to_c, to_s = line // 32 % 4, line // 16 % 2, line // 4 % 4
    to_v = to_f * (1 + 3 * c) + to_s * (4 - 3 * c)
    origin = (line // 128 * 2 + to_c) * per_group + to_v * 4 + line % 4
    moved = (iota((2 * n_rows, 2 * n_rows), 1) == origin).astype(F32).astype(BF16)
    selt[...] = dot_t(moved, sel[...]).astype(BF16)
    for copy in head_copies:
        copy.wait()

    def push(slot, q, j):
        return remote(
            rows.at[c, slot],
            rows.at[c, slot],
            ring_send.at[q, j],
            ring_recv.at[slot],
            vocab=vid(0, (1, 3, 2)[j]),
        )

    def share(model, slot):
        return remote(
            rows.at[model, slot],
            rows.at[model, slot],
            sib_send.at[slot],
            sib_recv.at[slot],
            dp=sibling,
        )

    def order(j):
        return jnp.where(j == 1, 1, jnp.where(j == 2, 3, jnp.where(j == 3, 2, 0)))

    def parts_step(q, carry):
        @pl.when(q < 4)
        def _():
            for j in range(1, GROUPS):
                other = (group + j) % GROUPS
                remote(
                    gath.at[q, other],
                    gath.at[q, other],
                    p1_send.at[q, 0],
                    p1_recv.at[q, other],
                    dp=other,
                ).wait_recv()
            local_copy(0, q).wait()

            @pl.when(q < 4 - AHEAD)
            def _():
                each_part(q, lambda copy: copy.wait_send())
                start_parts(q + AHEAD)

            slot = s * 4 + q
            packed = gath[q].reshape(GROUPS * per_group, part)
            rows[c, slot] = dot(sel[...], packed).astype(BF16)
            for j in range(3):
                push(slot, q, j).start()
            share(c, slot).start()

        @pl.when((q >= LAG) & (q < LAG + 4))
        def _():
            for j in range(3):
                slot = (s + (1, 3, 2)[j]) % 4 * 4 + q - LAG
                push(slot, 0, j).wait_recv()
                share(c, slot).start()

        def multiply(i, carry):
            own_part = i < 4
            back = jnp.where(i == 0, 0, jnp.where(own_part, LAG, LAG + 1))
            place = jnp.where(own_part, s + order(i), f + order(i - 4)) % 4
            slot = place * 4 + q - back
            model = jnp.where(own_part, c, 1 - c)

            @pl.when((q >= back) & (q < back + 4))
            def _():
                @pl.when(i >= 4)
                def _():
                    share(model, slot).wait_recv()

                at = pl.ds(pl.multiple_of(slot * part, part), part)
                acc[model] += dot(rows[model, slot], head[model, at, :])

            return carry

        lax.fori_loop(0, 8, multiply, 0)
        return carry

    lax.fori_loop(0, LAG + 5, parts_step, 0)

    def drain_ring():
        for q in range(4):
            for j in range(3):
                push(s * 4 + q, q, j).wait_send()
        for slot in range(PEERS):
            share(c, slot).wait_send()

    drains.append(drain_ring)

    chunks = shard // 128
    for m in (0, 1):
        for q in range(chunks):
            at = slice(q * 128, (q + 1) * 128)
            logt[m, at, :] = jnp.transpose(acc[m, :, at])
    top_p = jnp.max(logt[0], axis=0, keepdims=True)
    top_r = jnp.max(logt[1], axis=0, keepdims=True)
    step = 32
    zero = jnp.zeros((8, n_rows), F32)

    def fold(value):
        return jnp.sum(value.reshape(step // 8, 8, n_rows), axis=0)

    def local_sums(q, carry):
        s0, s1, s2, r0, r1 = carry
        at = pl.ds(pl.multiple_of(q * step, step), step)
        lp = logt[0, at, :] - top_p
        lr = logt[1, at, :] - top_r
        ep, er = jnp.exp(lp), jnp.exp(lr)
        d = lp - lr
        ed = ep * d
        return (
            s0 + fold(ep),
            s1 + fold(ed),
            s2 + fold(ed * d),
            r0 + fold(er),
            r1 + fold(er * d),
        )

    sums = lax.fori_loop(0, shard // step, local_sums, (zero,) * 5)
    sums = [jnp.sum(value, axis=0, keepdims=True) for value in sums]
    blank = jnp.zeros((1, n_rows), F32)
    stat_d[group] = jnp.concatenate([top_p, top_r, *sums, blank], axis=0)
    for j in range(1, GROUPS):
        remote(
            stat_d.at[group],
            stat_d.at[group],
            sd_send.at[j],
            sd_recv.at[group],
            dp=(group + j) % GROUPS,
        ).start()
    for ds in (1, 2, 3):
        pl.semaphore_signal(token, inc=1, device_id={"vocab": vid(0, ds)}, device_id_type=MESH)
    for j in range(1, GROUPS):
        other = (group + j) % GROUPS
        remote(
            stat_d.at[other], stat_d.at[other], sd_send.at[j], sd_recv.at[other], dp=other
        ).wait_recv()
    pl.semaphore_wait(token, 3)

    def drain_stat_d():
        for j in range(1, GROUPS):
            remote(
                stat_d.at[group],
                stat_d.at[group],
                sd_send.at[j],
                sd_recv.at[group],
                dp=(group + j) % GROUPS,
            ).wait_send()

    drains.append(drain_stat_d)
    stat_v[v] = jnp.concatenate([*merge_stats(stat_d), blank], axis=0)
    for j in range(1, PEERS):
        remote(
            stat_v.at[v], stat_v.at[v], sv_send.at[j], sv_recv.at[v], vocab=(v + j) % PEERS
        ).start()
    for j in range(1, PEERS):
        other = (v + j) % PEERS
        remote(
            stat_v.at[other], stat_v.at[other], sv_send.at[j], sv_recv.at[other], vocab=other
        ).wait_recv()

    def drain_stat_v():
        for j in range(1, PEERS):
            remote(
                stat_v.at[v], stat_v.at[v], sv_send.at[j], sv_recv.at[v], vocab=(v + j) % PEERS
            ).wait_send()

    drains.append(drain_stat_v)
    top_p, top_r, s0, s1, s2, r0, r1 = merge_stats(stat_v)
    log_s, log_r = jnp.log(s0), jnp.log(r0)
    norm_p, norm_r = top_p + log_s, top_r + log_r
    move = log_r - log_s
    forward = s1 / s0 + move
    squared = 0.5 * ((s2 + move * (2.0 * s1)) / s0 + move * move)
    reverse = -(r1 / r0 + move)
    both = forward + squared
    weight = float(SPAN) / length_row[0:1, :]

    def slopes(q, carry):
        at = pl.ds(pl.multiple_of(q * step, step), step)
        lp = logt[0, at, :] - norm_p
        d = lp - (logt[1, at, :] - norm_r)
        slope[at, :] = (weight * jnp.exp(lp) * (0.5 * d * d + d - both)).astype(BF16)
        return carry

    lax.fori_loop(0, shard // step, slopes, 0)

    chunk = half // 4
    order_s = (2, 1, 3, 0)

    def start_of(core, index):
        return pl.multiple_of(core * half + index * chunk, chunk)

    def a_copy(t):
        return remote(a_src.at[t], a_dst.at[t], a_send.at[t], a_recv.at[t], dp=sibling)

    def b_copy(t):
        return remote(
            b_src.at[t], b_dst.at[t], b_send.at[t], b_recv.at[t], vocab=vid(0, order_s[t])
        )

    def theirs(t):
        at = start_of(1 - c, (f + order_s[t]) % 4)
        a_src[t] = dot(head[0, pl.ds(at, chunk), :], slope[...]).astype(BF16)
        a_copy(t).start()

    def mine(t):
        at = start_of(c, (s + order_s[t]) % 4)
        own[...] = dot(head[0, pl.ds(at, chunk), :], slope[...])

    theirs(0)
    for t in range(3):
        mine(t)
        theirs(t + 1)
        a_copy(t).wait_recv()
        b_src[t] = (own[...] + a_dst[t].astype(F32)).astype(BF16)
        b_copy(t).start()
    mine(3)
    a_copy(3).wait_recv()
    total = own[...] + a_dst[3].astype(F32)
    for t in range(3):
        b_copy(t).wait_recv()
        total = total + b_dst[t].astype(F32)

    def drain_b():
        for t in range(4):
            a_copy(t).wait_send()
        for t in range(3):
            b_copy(t).wait_send()

    drains.append(drain_b)

    spread = dot_t(selt[...], total.astype(BF16)).astype(BF16)
    c_src[...] = spread.reshape(PEERS, 32, chunk)
    here = y * 4 + f

    def c_copy(j, arriving):
        to_y, to_f = (y + j // 4) % 4, (f + j % 4) % 4
        other = to_y * 4 + to_f
        return remote(
            c_src.at[other],
            c_dst.at[other if arriving else here],
            c_send.at[j],
            c_recv.at[other if arriving else here],
            dp=2 * to_y + c,
            vocab=vid(j % 4, 0),
        )

    order_c = (10, 6, 9, 11, 14, 2, 8, 5, 7, 13, 15, 1, 3, 4, 12)
    for j in order_c:
        c_copy(j, False).start()
    c_dst[here] = c_src[here]

    stacked = jnp.concatenate([forward, squared, reverse], axis=0)
    share_rows = n_rows // GROUPS
    result = jnp.zeros((3, share_rows), F32)
    for j in range(GROUPS):
        result = jnp.where(group == j, stacked[:, j * share_rows : (j + 1) * share_rows], result)
    div_out[...] = result

    for j in order_c:
        c_copy(j, True).wait_recv()
    value = c_dst[0].astype(F32)
    for k in range(1, PEERS):
        value = value + c_dst[k].astype(F32)
    d_src[...] = value

    def drain_c():
        for j in order_c:
            c_copy(j, False).wait_send()

    drains.append(drain_c)

    def d_copy(dc, ds, arriving):
        to_c, to_s = (c + dc) % 2, (s + ds) % 4
        at = pl.multiple_of(to_c * 16 + to_s // 2 * 8, 8)
        return remote(
            d_src.at[pl.ds(at, 8)],
            d_dst.at[c * 4 + s],
            d_send.at[dc * 4 + ds],
            d_recv.at[c * 4 + s],
            dp=2 * y + to_c,
            vocab=vid(0, ds),
        )

    others = [(dc, ds) for ds in (2, 1, 3, 0) for dc in (0, 1) if (dc, ds) != (0, 0)]
    for dc, ds in others:
        d_copy(dc, ds, False).start()
    d_dst[c * 4 + s] = d_src[pl.ds(pl.multiple_of(c * 16 + s // 2 * 8, 8), 8), :]
    for slot in range(GROUPS):

        @pl.when(slot != c * 4 + s)
        def _():
            remote(
                d_src.at[pl.ds(0, 8)],
                d_dst.at[slot],
                d_send.at[0],
                d_recv.at[slot],
                dp=sibling,
            ).wait_recv()

    for u in range(GROUPS):
        odd = (z, x)[u // 4] % 2 == 1
        grad_out[:, u * chunk : (u + 1) * chunk] = jnp.where(
            odd, d_dst[u, 4:8, :], d_dst[u, 0:4, :]
        )

    def drain_d():
        for dc, ds in others:
            d_copy(dc, ds, False).wait_send()

    drains.append(drain_d)
    finish()


def body(pol_hidden, ref_hidden, pol_head, ref_head, kept, send_counts, lengths):
    per_group, width = pol_hidden.shape
    shard = pol_head.shape[1]
    n_rows = GROUPS * per_group // 2
    part = width // PEERS
    chunk = width // 8
    vmem = pl.BlockSpec(memory_space=pltpu.VMEM)
    hbm = pl.BlockSpec(memory_space=pl.ANY)
    dma = pltpu.SemaphoreType.DMA
    return pl.pallas_call(
        kernel,
        out_shape=(
            jax.ShapeDtypeStruct((3, n_rows // GROUPS), F32),
            jax.ShapeDtypeStruct((4, width), F32),
        ),
        in_specs=[hbm, hbm, hbm, hbm, vmem, vmem, vmem],
        out_specs=(vmem, vmem),
        scratch_shapes=[
            pltpu.VMEM((2, width, shard), BF16),
            pltpu.VMEM((4, GROUPS, per_group, part), BF16),
            pltpu.VMEM((2, PEERS, n_rows, part), BF16),
            pltpu.VMEM((2, n_rows, shard), F32),
            pltpu.VMEM((2, shard, n_rows), F32),
            pltpu.VMEM((shard, n_rows), BF16),
            pltpu.VMEM((GROUPS, 8, 128), jnp.int32),
            pltpu.VMEM((n_rows, 2 * n_rows), BF16),
            pltpu.VMEM((2 * n_rows, n_rows), BF16),
            pltpu.VMEM((8, n_rows), F32),
            pltpu.VMEM((PEERS, 8, n_rows), F32),
            pltpu.VMEM((GROUPS, 8, n_rows), F32),
            pltpu.VMEM((4, chunk, n_rows), BF16),
            pltpu.VMEM((4, chunk, n_rows), BF16),
            pltpu.VMEM((chunk, n_rows), F32),
            pltpu.VMEM((3, chunk, n_rows), BF16),
            pltpu.VMEM((3, chunk, n_rows), BF16),
            pltpu.VMEM((PEERS, 32, chunk), BF16),
            pltpu.VMEM((PEERS, 32, chunk), BF16),
            pltpu.VMEM((32, chunk), F32),
            pltpu.VMEM((GROUPS, 8, chunk), F32),
            dma((2, 4)),
            dma((4,)),
            dma((4, 8)),
            dma((4, GROUPS)),
            dma((GROUPS,)),
            dma((GROUPS,)),
            dma((4, 3)),
            dma((PEERS,)),
            dma((PEERS,)),
            dma((PEERS,)),
            pltpu.SemaphoreType.REGULAR,
            dma((PEERS,)),
            dma((PEERS,)),
            dma((GROUPS,)),
            dma((GROUPS,)),
            dma((4,)),
            dma((4,)),
            dma((3,)),
            dma((3,)),
            dma((PEERS,)),
            dma((PEERS,)),
            dma((GROUPS,)),
            dma((GROUPS,)),
        ],
        compiler_params=pltpu.CompilerParams(
            collective_id=0, has_side_effects=True, vmem_limit_bytes=56 * 1024 * 1024
        ),
        cost_estimate=pl.CostEstimate(
            flops=6 * n_rows * width * shard, bytes_accessed=4 * width * shard, transcendentals=0
        ),
        name="divergence_heads",
    )(
        pol_hidden,
        ref_hidden,
        pol_head,
        ref_head,
        kept.reshape(1, per_group),
        send_counts,
        lengths.reshape(1, 2),
    )


def solution(mesh):
    return jax.shard_map(
        body,
        mesh=mesh,
        in_specs=(
            P("dp", None),
            P("dp", None),
            P(None, ("dp", "vocab")),
            P(None, ("dp", "vocab")),
            P("dp"),
            P("dp", None),
            P("dp"),
        ),
        out_specs=(P(None, "dp"), P(("dp", "vocab"), None)),
        check_vma=False,
    )
```

```python
import functools

import jax
import jax.numpy as jnp
from jax import lax
from jax.experimental import pallas as pl
from jax.experimental.pallas import tpu as pltpu
from jax.sharding import PartitionSpec as P

MESH = pl.DeviceIdType.MESH
GROUPS = 8
PEERS = 16
SPAN = 32
PIECES = 8
CUTS = 2
LAG = 3
AHEAD = 3
F32 = jnp.float32
BF16 = jnp.bfloat16


def dot(a, b):
    return lax.dot_general(a, b, (((1,), (0,)), ((), ())), preferred_element_type=F32)


def dot_t(a, b):
    return lax.dot_general(a, b, (((1,), (1,)), ((), ())), preferred_element_type=F32)


def iota(shape, axis):
    return lax.broadcasted_iota(jnp.int32, shape, axis)


def merge_stats(block):
    top_p, top_r = block[:, 0, :], block[:, 1, :]
    s0, s1, s2 = block[:, 2, :], block[:, 3, :], block[:, 4, :]
    r0, r1 = block[:, 5, :], block[:, 6, :]
    best_p = jnp.max(top_p, axis=0, keepdims=True)
    best_r = jnp.max(top_r, axis=0, keepdims=True)
    low_p, low_r = top_p - best_p, top_r - best_r
    shift = low_p - low_r
    scale_p, scale_r = jnp.exp(low_p), jnp.exp(low_r)

    def total(value):
        return jnp.sum(value, axis=0, keepdims=True)

    return (
        best_p,
        best_r,
        total(scale_p * s0),
        total(scale_p * (s1 + shift * s0)),
        total(scale_p * (s2 + shift * (2.0 * s1 + shift * s0))),
        total(scale_r * r0),
        total(scale_r * (r1 + shift * r0)),
    )


def kernel(
    pol_hidden,
    ref_hidden,
    pol_head,
    ref_head,
    kept,
    counts,
    lengths,
    out,
    head,
    gath,
    rows,
    acc,
    logt,
    slope,
    info,
    sel,
    selt,
    length_row,
    stat_v,
    stat_d,
    a_src,
    a_dst,
    own,
    b_src,
    b_dst,
    c_src,
    c_dst,
    d_src,
    d_dst,
    head_sem,
    local_sem,
    p1_send,
    p1_recv,
    info_send,
    info_recv,
    ring_send,
    ring_recv,
    sib_send,
    sib_recv,
    token,
    sv_send,
    sv_recv,
    sd_send,
    sd_recv,
    a_send,
    a_recv,
    b_send,
    b_recv,
    c_send,
    c_recv,
    d_send,
    d_recv,
):
    group = lax.axis_index("dp")
    v = lax.axis_index("vocab")
    y, c = group // 2, group % 2
    z, x = v // 4, v % 4
    f = x * (1 - c) + z * c
    s = z * (1 - c) + x * c
    per_group, width = pol_hidden.shape
    part = width // (4 * PIECES)
    half = width // 2
    shard = pol_head.shape[1]
    n_rows = rows.shape[2]

    def vid(df, ds):
        ff, ss = (f + df) % 4, (s + ds) % 4
        return ff * (1 + 3 * c) + ss * (4 - 3 * c)

    def remote(src, dst, send, recv, dp=None, vocab=None):
        target = {}
        if dp is not None:
            target["dp"] = dp
        if vocab is not None:
            target["vocab"] = vocab
        return pltpu.make_async_remote_copy(
            src_ref=src,
            dst_ref=dst,
            send_sem=send,
            recv_sem=recv,
            device_id=target,
            device_id_type=MESH,
        )

    sibling = group + 1 - 2 * c
    drains = []

    def finish():
        while drains:
            drains.pop(0)()


    head_copies = []
    quarter = width // 4
    for m, source in enumerate((pol_head, ref_head)):
        for q in range(4):
            at = pl.ds(q * quarter, quarter)
            copy = pltpu.make_async_copy(source.at[at], head.at[m, at], head_sem.at[m, q])
            copy.start()
            head_copies.append(copy)
    barrier = pltpu.get_barrier_semaphore()
    for j in range(1, GROUPS):
        pl.semaphore_signal(
            barrier, inc=1, device_id={"dp": (group + j) % GROUPS}, device_id_type=MESH
        )
    for ds in (1, 2, 3):
        pl.semaphore_signal(
            barrier, inc=1, device_id={"vocab": vid(0, ds)}, device_id_type=MESH
        )
    info[group] = jnp.zeros(info.shape[1:], jnp.int32)
    info[group, 0:1, 0:per_group] = kept[...]
    info[group, 1:2, 0:GROUPS] = counts[...]
    info[group, 2:3, 0:2] = lengths[...]
    pl.semaphore_wait(barrier, GROUPS + 2)

    for j in range(1, GROUPS):
        remote(
            info.at[group],
            info.at[group],
            info_send.at[j],
            info_recv.at[group],
            dp=(group + j) % GROUPS,
        ).start()
    hiddens = (pol_hidden, ref_hidden)

    def part_source(m, q):
        at = pl.multiple_of(((z, x)[m] * PIECES + q) * part, part)
        return hiddens[m].at[:, pl.ds(at, part)]

    def part_copy(m, dy, q):
        return remote(
            part_source(m, q),
            gath.at[q, group],
            p1_send.at[q, 2 * dy + m],
            p1_recv.at[q, group],
            dp=2 * ((y + dy) % 4) + m,
        )

    def local_copy(m, q):
        return pltpu.make_async_copy(part_source(m, q), gath.at[q, group], local_sem.at[q])

    def each_part(q, act):
        for dy in (2, 1, 3):
            for m in (0, 1):
                act(part_copy(m, dy, q))
        for m in (0, 1):

            @pl.when(c != m)
            def _():
                act(part_copy(m, 0, q))

    def start_parts(q):
        each_part(q, lambda copy: copy.start())
        for m in (0, 1):

            @pl.when(c == m)
            def _():
                local_copy(m, q).start()

    for q in range(AHEAD):
        start_parts(q)

    acc[...] = jnp.zeros(acc.shape, F32)

    def drain_parts():
        for j in range(1, GROUPS):
            remote(
                info.at[group],
                info.at[group],
                info_send.at[j],
                info_recv.at[group],
                dp=(group + j) % GROUPS,
            ).wait_send()
        for q in range(PIECES - AHEAD, PIECES):
            each_part(q, lambda copy: copy.wait_send())

    drains.append(drain_parts)

    for j in range(1, GROUPS):
        other = (group + j) % GROUPS
        remote(
            info.at[other], info.at[other], info_send.at[j], info_recv.at[other], dp=other
        ).wait_recv()
    kept_g = jnp.concatenate([info[i, 0:1, :] for i in range(GROUPS)], axis=0).astype(F32)
    count_g = jnp.concatenate([info[i, 1:2, :] for i in range(GROUPS)], axis=0).astype(F32)
    length_g = jnp.concatenate([info[i, 2:3, :] for i in range(GROUPS)], axis=0).astype(F32)
    upper = (iota((128, 128), 0) < iota((128, 128), 1)).astype(F32)
    rank = dot(kept_g, upper)
    start = dot(count_g, upper)
    line = jnp.zeros((1, 128), F32)
    lines = []
    for i in range(GROUPS):
        lines.append(line)
        line = line + count_g[i : i + 1, :]
    offset = jnp.concatenate(lines, axis=0)
    placed = jnp.zeros((GROUPS, 128), F32)
    for j in range(GROUPS):
        first = start[:, j : j + 1]
        last = first + count_g[:, j : j + 1]
        target = float(j * (n_rows // GROUPS)) + offset[:, j : j + 1] + rank - first
        placed = placed + jnp.where((first <= rank) & (rank < last), target, 0.0)
    placed = jnp.where(kept_g > 0.5, placed, -1.0)
    lane = iota((GROUPS, 128), 1)
    length_g = jnp.where(lane < SPAN, length_g[:, 0:1], length_g[:, 1:2])
    length_g = jnp.where(kept_g > 0.5, length_g, 0.0)
    placed_r = pltpu.roll(placed, 64, 1)
    length_r = pltpu.roll(length_g, 64, 1)
    place = iota((n_rows, 128), 0).astype(F32)
    low = lane[0:1] < 64
    weight_len = jnp.zeros((8, n_rows), F32)
    for k in range(4):
        pair = jnp.where(low, placed[2 * k : 2 * k + 1], placed_r[2 * k + 1 : 2 * k + 2])
        spans = jnp.where(low, length_g[2 * k : 2 * k + 1], length_r[2 * k + 1 : 2 * k + 2])
        chosen = (place == pair).astype(F32)
        sel[:, k * 128 : (k + 1) * 128] = chosen.astype(BF16)
        weight_len = weight_len + dot_t(jnp.broadcast_to(spans, (8, 128)), chosen)
    length_row[...] = weight_len

    line = iota((2 * n_rows, 2 * n_rows), 0)
    to_f, to_c, to_s = line // 32 % 4, line // 16 % 2, line // 4 % 4
    to_v = to_f * (1 + 3 * c) + to_s * (4 - 3 * c)
    origin = (line // 128 * 2 + to_c) * per_group + to_v * 4 + line % 4
    moved = (iota((2 * n_rows, 2 * n_rows), 1) == origin).astype(F32).astype(BF16)
    selt[...] = dot_t(moved, sel[...]).astype(BF16)
    for copy in head_copies:
        copy.wait()

    def push(slot, q, j):
        return remote(
            rows.at[c, slot],
            rows.at[c, slot],
            ring_send.at[q, j],
            ring_recv.at[slot],
            vocab=vid(0, (1, 3, 2)[j]),
        )

    def share(model, slot):
        return remote(
            rows.at[model, slot],
            rows.at[model, slot],
            sib_send.at[slot],
            sib_recv.at[slot],
            dp=sibling,
        )

    def order(j):
        return jnp.where(j == 1, 1, jnp.where(j == 2, 3, jnp.where(j == 3, 2, 0)))

    def multiply(model, first, q):
        total = acc[model]
        for k in range(4):
            slot = ((first + k) % 4) * PIECES + 2 * q
            at = pl.ds(pl.multiple_of(slot * part, 2 * part), 2 * part)
            both = jnp.concatenate([rows[model, slot], rows[model, slot + 1]], axis=1)
            total = total + dot(both, head[model, at, :])
        acc[model] = total

    def parts_step(p, carry):
        @pl.when(p < PIECES)
        def _():
            for j in range(1, GROUPS):
                other = (group + j) % GROUPS
                remote(
                    gath.at[p, other],
                    gath.at[p, other],
                    p1_send.at[p, 0],
                    p1_recv.at[p, other],
                    dp=other,
                ).wait_recv()
            local_copy(0, p).wait()

            @pl.when(p < PIECES - AHEAD)
            def _():
                each_part(p, lambda copy: copy.wait_send())
                start_parts(p + AHEAD)

            slot = s * PIECES + p
            packed = gath[p].reshape(GROUPS * per_group, part)
            rows[c, slot] = dot(sel[...], packed).astype(BF16)
            for j in range(3):
                push(slot, p, j).start()
            share(c, slot).start()

        def side(i, carry):
            t = p - LAG - 1 + i
            mine = i == 1
            first = jnp.where(mine, s, f)
            model = jnp.where(mine, c, 1 - c)

            @pl.when((t >= 0) & (t < PIECES))
            def _():
                @pl.when(mine)
                def _():
                    for j in range(3):
                        slot = (s + (1, 3, 2)[j]) % 4 * PIECES + t
                        push(slot, 0, j).wait_recv()
                        share(c, slot).start()

                @pl.when(t % 2 == 1)
                def _():
                    @pl.when(i == 0)
                    def _():
                        for k in range(4):
                            for e in (1, 0):
                                slot = (f + k) % 4 * PIECES + t - e
                                share(1 - c, slot).wait_recv()

                    multiply(model, first, t // 2)

            return carry

        lax.fori_loop(0, 2, side, 0)
        return carry

    lax.fori_loop(0, PIECES + LAG + 1, parts_step, 0)

    def drain_ring():
        for p in range(PIECES):
            for j in range(3):
                push(s * PIECES + p, p, j).wait_send()
        for slot in range(4 * PIECES):
            share(c, slot).wait_send()

    drains.append(drain_ring)

    chunks = shard // 128
    for m in (0, 1):
        for q in range(chunks):
            at = slice(q * 128, (q + 1) * 128)
            logt[m, at, :] = jnp.transpose(acc[m, :, at])
    top_p = jnp.max(logt[0], axis=0, keepdims=True)
    top_r = jnp.max(logt[1], axis=0, keepdims=True)
    step = 32
    zero = jnp.zeros((8, n_rows), F32)

    def fold(value):
        return jnp.sum(value.reshape(step // 8, 8, n_rows), axis=0)

    def local_sums(q, carry):
        s0, s1, s2, r0, r1 = carry
        at = pl.ds(pl.multiple_of(q * step, step), step)
        lp = logt[0, at, :] - top_p
        lr = logt[1, at, :] - top_r
        ep, er = jnp.exp(lp), jnp.exp(lr)
        d = lp - lr
        ed = ep * d
        return (
            s0 + fold(ep),
            s1 + fold(ed),
            s2 + fold(ed * d),
            r0 + fold(er),
            r1 + fold(er * d),
        )

    sums = lax.fori_loop(0, shard // step, local_sums, (zero,) * 5)
    sums = [jnp.sum(value, axis=0, keepdims=True) for value in sums]
    blank = jnp.zeros((1, n_rows), F32)
    stat_d[group] = jnp.concatenate([top_p, top_r, *sums, blank], axis=0)
    for j in range(1, GROUPS):
        remote(
            stat_d.at[group],
            stat_d.at[group],
            sd_send.at[j],
            sd_recv.at[group],
            dp=(group + j) % GROUPS,
        ).start()
    for ds in (1, 2, 3):
        pl.semaphore_signal(token, inc=1, device_id={"vocab": vid(0, ds)}, device_id_type=MESH)
    for j in range(1, GROUPS):
        other = (group + j) % GROUPS
        remote(
            stat_d.at[other], stat_d.at[other], sd_send.at[j], sd_recv.at[other], dp=other
        ).wait_recv()
    pl.semaphore_wait(token, 3)

    def drain_stat_d():
        for j in range(1, GROUPS):
            remote(
                stat_d.at[group],
                stat_d.at[group],
                sd_send.at[j],
                sd_recv.at[group],
                dp=(group + j) % GROUPS,
            ).wait_send()

    drains.append(drain_stat_d)
    stat_v[v] = jnp.concatenate([*merge_stats(stat_d), blank], axis=0)
    for j in range(1, PEERS):
        remote(
            stat_v.at[v], stat_v.at[v], sv_send.at[j], sv_recv.at[v], vocab=(v + j) % PEERS
        ).start()
    finish()
    for j in range(1, PEERS):
        other = (v + j) % PEERS
        remote(
            stat_v.at[other], stat_v.at[other], sv_send.at[j], sv_recv.at[other], vocab=other
        ).wait_recv()

    def drain_stat_v():
        for j in range(1, PEERS):
            remote(
                stat_v.at[v], stat_v.at[v], sv_send.at[j], sv_recv.at[v], vocab=(v + j) % PEERS
            ).wait_send()

    drains.append(drain_stat_v)
    top_p, top_r, s0, s1, s2, r0, r1 = merge_stats(stat_v)
    log_s, log_r = jnp.log(s0), jnp.log(r0)
    norm_p, norm_r = top_p + log_s, top_r + log_r
    move = log_r - log_s
    forward = s1 / s0 + move
    squared = 0.5 * ((s2 + move * (2.0 * s1)) / s0 + move * move)
    reverse = -(r1 / r0 + move)
    both = forward + squared
    weight = float(SPAN) / length_row[0:1, :]

    def slopes(q, carry):
        at = pl.ds(pl.multiple_of(q * step, step), step)
        lp = logt[0, at, :] - norm_p
        d = lp - (logt[1, at, :] - norm_r)
        slope[at, :] = (weight * jnp.exp(lp) * (0.5 * d * d + d - both)).astype(BF16)
        return carry

    lax.fori_loop(0, shard // step, slopes, 0)

    chunk = half // 4
    order_s = (2, 1, 3, 0)

    cut = chunk // CUTS

    def start_of(core, index, h):
        return pl.multiple_of(core * half + index * chunk + h * cut, cut)

    def a_copy(h, t):
        return remote(
            a_src.at[h, t], a_dst.at[h, t], a_send.at[h, t], a_recv.at[h, t], dp=sibling
        )

    def b_copy(h, t):
        return remote(
            b_src.at[h, t],
            b_dst.at[h, t],
            b_send.at[h, t],
            b_recv.at[h, t],
            vocab=vid(0, order_s[t]),
        )

    def gradient(h, carry):
        def theirs(t):
            at = start_of(1 - c, (f + order_s[t]) % 4, h)
            a_src[h, t] = dot(head[0, pl.ds(at, cut), :], slope[...]).astype(BF16)
            a_copy(h, t).start()

        def mine(t):
            at = start_of(c, (s + order_s[t]) % 4, h)
            own[h] = dot(head[0, pl.ds(at, cut), :], slope[...])

        for t in range(4):
            theirs(t)
        for t in range(3):
            mine(t)
            a_copy(h, t).wait_recv()
            b_src[h, t] = (own[h] + a_dst[h, t].astype(F32)).astype(BF16)
            b_copy(h, t).start()
        mine(3)
        a_copy(h, 3).wait_recv()
        own[h] = own[h] + a_dst[h, 3].astype(F32)
        return carry

    lax.fori_loop(0, CUTS, gradient, 0)

    def drain_b():
        for h in range(CUTS):
            for t in range(4):
                a_copy(h, t).wait_send()
            for t in range(3):
                b_copy(h, t).wait_send()

    drains.append(drain_b)

    here = y * 4 + f

    def c_copy(h, j, arriving):
        to_y, to_f = (y + j // 4) % 4, (f + j % 4) % 4
        other = to_y * 4 + to_f
        return remote(
            c_src.at[h, other],
            c_dst.at[h, other if arriving else here],
            c_send.at[h, j],
            c_recv.at[h, other if arriving else here],
            dp=2 * to_y + c,
            vocab=vid(j % 4, 0),
        )

    order_c = (10, 6, 9, 11, 14, 2, 8, 5, 7, 13, 15, 1, 3, 4, 12)
    for h in range(CUTS):
        total = own[h]
        for t in range(3):
            b_copy(h, t).wait_recv()
            total = total + b_dst[h, t].astype(F32)
        spread = dot_t(selt[...], total.astype(BF16)).astype(BF16)
        c_src[h] = spread.reshape(PEERS, 32, cut)
        for j in order_c:
            c_copy(h, j, False).start()

    finish()
    stacked = jnp.concatenate([forward, squared, reverse], axis=0)
    share_rows = n_rows // GROUPS
    result = jnp.zeros((3, share_rows), F32)
    for j in range(GROUPS):
        result = jnp.where(group == j, stacked[:, j * share_rows : (j + 1) * share_rows], result)
    out[4:7, 0:share_rows] = result

    for h in range(CUTS):
        c_dst[h, here] = c_src[h, here]
        for j in order_c:
            c_copy(h, j, True).wait_recv()
        value = c_dst[h, 0].astype(F32)
        for k in range(1, PEERS):
            value = value + c_dst[h, k].astype(F32)
        d_src[:, h * cut : (h + 1) * cut] = value

    def drain_c():
        for h in range(CUTS):
            for j in order_c:
                c_copy(h, j, False).wait_send()

    drains.append(drain_c)

    def d_copy(dc, ds, arriving):
        to_c, to_s = (c + dc) % 2, (s + ds) % 4
        at = pl.multiple_of(to_c * 16 + to_s // 2 * 8, 8)
        return remote(
            d_src.at[pl.ds(at, 8)],
            d_dst.at[c * 4 + s],
            d_send.at[dc * 4 + ds],
            d_recv.at[c * 4 + s],
            dp=2 * y + to_c,
            vocab=vid(0, ds),
        )

    others = [(dc, ds) for ds in (2, 1, 3, 0) for dc in (0, 1) if (dc, ds) != (0, 0)]
    for dc, ds in others:
        d_copy(dc, ds, False).start()
    finish()
    d_dst[c * 4 + s] = d_src[pl.ds(pl.multiple_of(c * 16 + s // 2 * 8, 8), 8), :]
    for slot in range(GROUPS):

        @pl.when(slot != c * 4 + s)
        def _():
            remote(
                d_src.at[pl.ds(0, 8)],
                d_dst.at[slot],
                d_send.at[0],
                d_recv.at[slot],
                dp=sibling,
            ).wait_recv()

    for u in range(GROUPS):
        odd = (z, x)[u // 4] % 2 == 1
        out[0:4, u * chunk : (u + 1) * chunk] = jnp.where(
            odd, d_dst[u, 4:8, :], d_dst[u, 0:4, :]
        )

    def drain_d():
        for dc, ds in others:
            d_copy(dc, ds, False).wait_send()

    drains.append(drain_d)
    finish()


def split(both, div_out, grad_out):
    div_out[...] = both[4:7, 0 : div_out.shape[1]]
    grad_out[...] = both[0:4, :]


def body(pol_hidden, ref_hidden, pol_head, ref_head, kept, send_counts, lengths):
    per_group, width = pol_hidden.shape
    shard = pol_head.shape[1]
    n_rows = GROUPS * per_group // 2
    part = width // (4 * PIECES)
    chunk = width // 8
    cut = chunk // CUTS
    vmem = pl.BlockSpec(memory_space=pltpu.VMEM)
    hbm = pl.BlockSpec(memory_space=pl.ANY)
    dma = pltpu.SemaphoreType.DMA
    both = pl.pallas_call(
        kernel,
        out_shape=jax.ShapeDtypeStruct((8, width), F32),
        in_specs=[hbm, hbm, hbm, hbm, vmem, vmem, vmem],
        out_specs=vmem,
        scratch_shapes=[
            pltpu.VMEM((2, width, shard), BF16),
            pltpu.VMEM((PIECES, GROUPS, per_group, part), BF16),
            pltpu.VMEM((2, 4 * PIECES, n_rows, part), BF16),
            pltpu.VMEM((2, n_rows, shard), F32),
            pltpu.VMEM((2, shard, n_rows), F32),
            pltpu.VMEM((shard, n_rows), BF16),
            pltpu.VMEM((GROUPS, 8, 128), jnp.int32),
            pltpu.VMEM((n_rows, 2 * n_rows), BF16),
            pltpu.VMEM((2 * n_rows, n_rows), BF16),
            pltpu.VMEM((8, n_rows), F32),
            pltpu.VMEM((PEERS, 8, n_rows), F32),
            pltpu.VMEM((GROUPS, 8, n_rows), F32),
            pltpu.VMEM((CUTS, 4, cut, n_rows), BF16),
            pltpu.VMEM((CUTS, 4, cut, n_rows), BF16),
            pltpu.VMEM((CUTS, cut, n_rows), F32),
            pltpu.VMEM((CUTS, 3, cut, n_rows), BF16),
            pltpu.VMEM((CUTS, 3, cut, n_rows), BF16),
            pltpu.VMEM((CUTS, PEERS, 32, cut), BF16),
            pltpu.VMEM((CUTS, PEERS, 32, cut), BF16),
            pltpu.VMEM((32, chunk), F32),
            pltpu.VMEM((GROUPS, 8, chunk), F32),
            dma((2, 4)),
            dma((PIECES,)),
            dma((PIECES, 8)),
            dma((PIECES, GROUPS)),
            dma((GROUPS,)),
            dma((GROUPS,)),
            dma((PIECES, 3)),
            dma((4 * PIECES,)),
            dma((4 * PIECES,)),
            dma((4 * PIECES,)),
            pltpu.SemaphoreType.REGULAR,
            dma((PEERS,)),
            dma((PEERS,)),
            dma((GROUPS,)),
            dma((GROUPS,)),
            dma((CUTS, 4)),
            dma((CUTS, 4)),
            dma((CUTS, 3)),
            dma((CUTS, 3)),
            dma((CUTS, PEERS)),
            dma((CUTS, PEERS)),
            dma((GROUPS,)),
            dma((GROUPS,)),
        ],
        compiler_params=pltpu.CompilerParams(
            collective_id=0, has_side_effects=True, vmem_limit_bytes=56 * 1024 * 1024
        ),
        cost_estimate=pl.CostEstimate(
            flops=6 * n_rows * width * shard, bytes_accessed=4 * width * shard, transcendentals=0
        ),
        name="divergence_heads",
    )(
        pol_hidden,
        ref_hidden,
        pol_head,
        ref_head,
        kept.reshape(1, per_group),
        send_counts,
        lengths.reshape(1, 2),
    )
    return pl.pallas_call(
        split,
        out_shape=(
            jax.ShapeDtypeStruct((3, n_rows // GROUPS), F32),
            jax.ShapeDtypeStruct((4, width), F32),
        ),
        in_specs=[vmem],
        out_specs=(vmem, vmem),
        name="split_outputs",
    )(both)


def solution(mesh):
    return jax.shard_map(
        body,
        mesh=mesh,
        in_specs=(
            P("dp", None),
            P("dp", None),
            P(None, ("dp", "vocab")),
            P(None, ("dp", "vocab")),
            P("dp"),
            P("dp", None),
            P("dp"),
        ),
        out_specs=(P(None, "dp"), P(("dp", "vocab"), None)),
        check_vma=False,
    )
```

```python
import functools

import jax
import jax.numpy as jnp
from jax import lax
from jax.experimental import pallas as pl
from jax.experimental.pallas import tpu as pltpu
from jax.sharding import PartitionSpec as P

MESH = pl.DeviceIdType.MESH
GROUPS = 8
PEERS = 16
SPAN = 32
PIECES = 8
CUTS = 1
LAG = 3
F32 = jnp.float32
BF16 = jnp.bfloat16


def dot(a, b):
    return lax.dot_general(a, b, (((1,), (0,)), ((), ())), preferred_element_type=F32)


def dot_t(a, b):
    return lax.dot_general(a, b, (((1,), (1,)), ((), ())), preferred_element_type=F32)


def iota(shape, axis):
    return lax.broadcasted_iota(jnp.int32, shape, axis)


def merge_stats(block):
    top_p, top_r = block[:, 0, :], block[:, 1, :]
    s0, s1, s2 = block[:, 2, :], block[:, 3, :], block[:, 4, :]
    r0, r1 = block[:, 5, :], block[:, 6, :]
    best_p = jnp.max(top_p, axis=0, keepdims=True)
    best_r = jnp.max(top_r, axis=0, keepdims=True)
    low_p, low_r = top_p - best_p, top_r - best_r
    shift = low_p - low_r
    scale_p, scale_r = jnp.exp(low_p), jnp.exp(low_r)

    def total(value):
        return jnp.sum(value, axis=0, keepdims=True)

    return (
        best_p,
        best_r,
        total(scale_p * s0),
        total(scale_p * (s1 + shift * s0)),
        total(scale_p * (s2 + shift * (2.0 * s1 + shift * s0))),
        total(scale_r * r0),
        total(scale_r * (r1 + shift * r0)),
    )


def kernel(
    pol_hidden,
    ref_hidden,
    pol_head,
    ref_head,
    kept,
    counts,
    lengths,
    out,
    head,
    gath,
    rows,
    acc,
    logt,
    slope,
    info,
    sel,
    selt,
    length_row,
    stat_v,
    stat_d,
    a_src,
    a_dst,
    own,
    b_src,
    b_dst,
    c_src,
    c_dst,
    d_src,
    d_dst,
    head_sem,
    p1_send,
    p1_recv,
    info_send,
    info_recv,
    ring_send,
    ring_recv,
    sib_send,
    sib_recv,
    token,
    sv_send,
    sv_recv,
    sd_send,
    sd_recv,
    a_send,
    a_recv,
    b_send,
    b_recv,
    c_send,
    c_recv,
    d_send,
    d_recv,
):
    group = lax.axis_index("dp")
    v = lax.axis_index("vocab")
    y, c = group // 2, group % 2
    z, x = v // 4, v % 4
    f = x * (1 - c) + z * c
    s = z * (1 - c) + x * c
    per_group, width = pol_hidden.shape
    part = width // (4 * PIECES)
    half = width // 2
    shard = pol_head.shape[1]
    n_rows = rows.shape[2]

    def vid(df, ds):
        ff, ss = (f + df) % 4, (s + ds) % 4
        return ff * (1 + 3 * c) + ss * (4 - 3 * c)

    def remote(src, dst, send, recv, dp=None, vocab=None):
        target = {}
        if dp is not None:
            target["dp"] = dp
        if vocab is not None:
            target["vocab"] = vocab
        return pltpu.make_async_remote_copy(
            src_ref=src,
            dst_ref=dst,
            send_sem=send,
            recv_sem=recv,
            device_id=target,
            device_id_type=MESH,
        )

    sibling = group + 1 - 2 * c

    def await_in(like, sem):
        remote(like, like, sem, sem, dp=sibling).wait_recv()

    def await_out(like, sem):
        remote(like, like, sem, sem, dp=sibling).wait_send()

    drains = []

    def finish():
        while drains:
            drains.pop(0)()


    quarter = width // 4
    for m, source in enumerate((pol_head, ref_head)):
        for q in range(4):
            at = pl.ds(q * quarter, quarter)
            pltpu.make_async_copy(source.at[at], head.at[m, at], head_sem.at[0]).start()
    barrier = pltpu.get_barrier_semaphore()
    for j in range(1, GROUPS):
        pl.semaphore_signal(
            barrier, inc=1, device_id={"dp": (group + j) % GROUPS}, device_id_type=MESH
        )
    for ds in (1, 2, 3):
        pl.semaphore_signal(
            barrier, inc=1, device_id={"vocab": vid(0, ds)}, device_id_type=MESH
        )
    info[group] = jnp.zeros(info.shape[1:], jnp.int32)
    info[group, 0:1, 0:per_group] = kept[...]
    info[group, 1:2, 0:GROUPS] = counts[...]
    info[group, 2:3, 0:2] = lengths[...]
    pl.semaphore_wait(barrier, GROUPS + 2)

    for j in range(1, GROUPS):
        remote(
            info.at[group],
            info.at[group],
            info_send.at[0],
            info_recv.at[0],
            dp=(group + j) % GROUPS,
        ).start()
    hiddens = (pol_hidden, ref_hidden)

    def part_source(m, q):
        at = pl.multiple_of(((z, x)[m] * PIECES + q) * part, part)
        return hiddens[m].at[:, pl.ds(at, part)]

    def part_copy(m, dy, q):
        return remote(
            part_source(m, q),
            gath.at[q, group],
            p1_send.at[0],
            p1_recv.at[q],
            dp=2 * ((y + dy) % 4) + m,
        )

    def local_copy(m, q):
        return pltpu.make_async_copy(part_source(m, q), gath.at[q, group], p1_recv.at[q])

    def each_part(q, act):
        for dy in (2, 1, 3):
            for m in (0, 1):
                act(part_copy(m, dy, q))
        for m in (0, 1):

            @pl.when(c != m)
            def _():
                act(part_copy(m, 0, q))

    def start_parts(q):
        each_part(q, lambda copy: copy.start())
        for m in (0, 1):

            @pl.when(c == m)
            def _():
                local_copy(m, q).start()

    for q in range(PIECES):
        start_parts(q)

    acc[...] = jnp.zeros(acc.shape, F32)

    def drain_parts():
        await_out(info.at[pl.ds(0, GROUPS - 1)], info_send.at[0])
        for q in range(PIECES):
            await_out(gath.at[q, pl.ds(0, GROUPS - 1)], p1_send.at[0])

    drains.append(drain_parts)

    await_in(info.at[pl.ds(0, GROUPS - 1)], info_recv.at[0])
    kept_g = jnp.concatenate([info[i, 0:1, :] for i in range(GROUPS)], axis=0).astype(F32)
    count_g = jnp.concatenate([info[i, 1:2, :] for i in range(GROUPS)], axis=0).astype(F32)
    length_g = jnp.concatenate([info[i, 2:3, :] for i in range(GROUPS)], axis=0).astype(F32)
    upper = (iota((128, 128), 0) < iota((128, 128), 1)).astype(F32)
    rank = dot(kept_g, upper)
    start = dot(count_g, upper)
    line = jnp.zeros((1, 128), F32)
    lines = []
    for i in range(GROUPS):
        lines.append(line)
        line = line + count_g[i : i + 1, :]
    offset = jnp.concatenate(lines, axis=0)
    placed = jnp.zeros((GROUPS, 128), F32)
    for j in range(GROUPS):
        first = start[:, j : j + 1]
        last = first + count_g[:, j : j + 1]
        target = float(j * (n_rows // GROUPS)) + offset[:, j : j + 1] + rank - first
        placed = placed + jnp.where((first <= rank) & (rank < last), target, 0.0)
    placed = jnp.where(kept_g > 0.5, placed, -1.0)
    lane = iota((GROUPS, 128), 1)
    length_g = jnp.where(lane < SPAN, length_g[:, 0:1], length_g[:, 1:2])
    length_g = jnp.where(kept_g > 0.5, length_g, 0.0)
    placed_r = pltpu.roll(placed, 64, 1)
    length_r = pltpu.roll(length_g, 64, 1)
    place = iota((n_rows, 128), 0).astype(F32)
    low = lane[0:1] < 64
    weight_len = jnp.zeros((8, n_rows), F32)
    for k in range(4):
        pair = jnp.where(low, placed[2 * k : 2 * k + 1], placed_r[2 * k + 1 : 2 * k + 2])
        spans = jnp.where(low, length_g[2 * k : 2 * k + 1], length_r[2 * k + 1 : 2 * k + 2])
        chosen = (place == pair).astype(F32)
        sel[:, k * 128 : (k + 1) * 128] = chosen.astype(BF16)
        weight_len = weight_len + dot_t(jnp.broadcast_to(spans, (8, 128)), chosen)
    length_row[...] = weight_len

    line = iota((2 * n_rows, 2 * n_rows), 0)
    to_f, to_c, to_s = line // 32 % 4, line // 16 % 2, line // 4 % 4
    to_v = to_f * (1 + 3 * c) + to_s * (4 - 3 * c)
    origin = (line // 128 * 2 + to_c) * per_group + to_v * 4 + line % 4
    moved = (iota((2 * n_rows, 2 * n_rows), 1) == origin).astype(F32).astype(BF16)
    selt[...] = dot_t(moved, sel[...]).astype(BF16)
    pltpu.make_async_copy(head, head, head_sem.at[0]).wait()

    def push(slot, q, j):
        return remote(
            rows.at[c, slot],
            rows.at[c, slot],
            ring_send.at[0],
            ring_recv.at[q],
            vocab=vid(0, (1, 3, 2)[j]),
        )

    def share(model, slot):
        return remote(
            rows.at[model, slot],
            rows.at[model, slot],
            sib_send.at[0],
            sib_recv.at[slot % PIECES // 2],
            dp=sibling,
        )

    def order(j):
        return jnp.where(j == 1, 1, jnp.where(j == 2, 3, jnp.where(j == 3, 2, 0)))

    def multiply(model, first, q):
        total = acc[model]
        for k in range(4):
            slot = ((first + k) % 4) * PIECES + 2 * q
            at = pl.ds(pl.multiple_of(slot * part, 2 * part), 2 * part)
            both = jnp.concatenate([rows[model, slot], rows[model, slot + 1]], axis=1)
            total = total + dot(both, head[model, at, :])
        acc[model] = total

    def parts_step(p, carry):
        @pl.when(p < PIECES)
        def _():
            await_in(gath.at[p], p1_recv.at[p])
            slot = s * PIECES + p
            packed = gath[p].reshape(GROUPS * per_group, part)
            rows[c, slot] = dot(sel[...], packed).astype(BF16)
            for j in range(3):
                push(slot, p, j).start()
            share(c, slot).start()

        def side(i, carry):
            t = p - LAG - 1 + i
            mine = i == 1
            first = jnp.where(mine, s, f)
            model = jnp.where(mine, c, 1 - c)

            @pl.when((t >= 0) & (t < PIECES))
            def _():
                @pl.when(mine)
                def _():
                    await_in(rows.at[c, pl.ds(0, 3)], ring_recv.at[t])
                    for j in range(3):
                        share(c, (s + 1 + j) % 4 * PIECES + t).start()

                @pl.when(t % 2 == 1)
                def _():
                    @pl.when(i == 0)
                    def _():
                        await_in(rows.at[1 - c, pl.ds(0, 8)], sib_recv.at[t // 2])

                    multiply(model, first, t // 2)

            return carry

        lax.fori_loop(0, 2, side, 0)
        return carry

    lax.fori_loop(0, PIECES + LAG + 1, parts_step, 0)

    def drain_ring():
        await_out(rows.at[0, pl.ds(0, 3 * PIECES)], ring_send.at[0])
        await_out(rows.at[0], sib_send.at[0])

    drains.append(drain_ring)

    chunks = shard // 128
    for m in (0, 1):
        for q in range(chunks):
            at = slice(q * 128, (q + 1) * 128)
            logt[m, at, :] = jnp.transpose(acc[m, :, at])
    top_p = jnp.max(logt[0], axis=0, keepdims=True)
    top_r = jnp.max(logt[1], axis=0, keepdims=True)
    step = 32
    zero = jnp.zeros((8, n_rows), F32)

    def fold(value):
        return jnp.sum(value.reshape(step // 8, 8, n_rows), axis=0)

    def local_sums(q, carry):
        s0, s1, s2, r0, r1 = carry
        at = pl.ds(pl.multiple_of(q * step, step), step)
        lp = logt[0, at, :] - top_p
        lr = logt[1, at, :] - top_r
        ep, er = jnp.exp(lp), jnp.exp(lr)
        d = lp - lr
        ed = ep * d
        return (
            s0 + fold(ep),
            s1 + fold(ed),
            s2 + fold(ed * d),
            r0 + fold(er),
            r1 + fold(er * d),
        )

    sums = lax.fori_loop(0, shard // step, local_sums, (zero,) * 5)
    sums = [jnp.sum(value, axis=0, keepdims=True) for value in sums]
    blank = jnp.zeros((1, n_rows), F32)
    stat_d[group] = jnp.concatenate([top_p, top_r, *sums, blank], axis=0)
    for j in range(1, GROUPS):
        remote(
            stat_d.at[group],
            stat_d.at[group],
            sd_send.at[0],
            sd_recv.at[0],
            dp=(group + j) % GROUPS,
        ).start()
    for ds in (1, 2, 3):
        pl.semaphore_signal(token, inc=1, device_id={"vocab": vid(0, ds)}, device_id_type=MESH)
    await_in(stat_d.at[pl.ds(0, GROUPS - 1)], sd_recv.at[0])
    pl.semaphore_wait(token, 3)

    def drain_stat_d():
        await_out(stat_d.at[pl.ds(0, GROUPS - 1)], sd_send.at[0])

    drains.append(drain_stat_d)
    stat_v[v] = jnp.concatenate([*merge_stats(stat_d), blank], axis=0)
    for j in range(1, PEERS):
        remote(
            stat_v.at[v], stat_v.at[v], sv_send.at[0], sv_recv.at[0], vocab=(v + j) % PEERS
        ).start()
    finish()
    await_in(stat_v.at[pl.ds(0, PEERS - 1)], sv_recv.at[0])

    def drain_stat_v():
        await_out(stat_v.at[pl.ds(0, PEERS - 1)], sv_send.at[0])

    drains.append(drain_stat_v)
    top_p, top_r, s0, s1, s2, r0, r1 = merge_stats(stat_v)
    log_s, log_r = jnp.log(s0), jnp.log(r0)
    norm_p, norm_r = top_p + log_s, top_r + log_r
    move = log_r - log_s
    forward = s1 / s0 + move
    squared = 0.5 * ((s2 + move * (2.0 * s1)) / s0 + move * move)
    reverse = -(r1 / r0 + move)
    both = forward + squared
    weight = float(SPAN) / length_row[0:1, :]

    def slopes(q, carry):
        at = pl.ds(pl.multiple_of(q * step, step), step)
        lp = logt[0, at, :] - norm_p
        d = lp - (logt[1, at, :] - norm_r)
        slope[at, :] = (weight * jnp.exp(lp) * (0.5 * d * d + d - both)).astype(BF16)
        return carry

    lax.fori_loop(0, shard // step, slopes, 0)

    chunk = half // 4
    order_s = (2, 1, 3, 0)

    cut = chunk // CUTS

    def start_of(core, index, h):
        return pl.multiple_of(core * half + index * chunk + h * cut, cut)

    def a_copy(h, t):
        return remote(
            a_src.at[h, t], a_dst.at[h, t], a_send.at[0], a_recv.at[h, t], dp=sibling
        )

    def b_copy(h, t):
        return remote(
            b_src.at[h, t],
            b_dst.at[h, t],
            b_send.at[0],
            b_recv.at[h],
            vocab=vid(0, order_s[t]),
        )

    def gradient(h, carry):
        def theirs(t):
            at = start_of(1 - c, (f + order_s[t]) % 4, h)
            a_src[h, t] = dot(head[0, pl.ds(at, cut), :], slope[...]).astype(BF16)
            a_copy(h, t).start()

        def mine(t):
            at = start_of(c, (s + order_s[t]) % 4, h)
            own[h] = dot(head[0, pl.ds(at, cut), :], slope[...])

        for t in range(4):
            theirs(t)
        for t in range(3):
            mine(t)
            a_copy(h, t).wait_recv()
            b_src[h, t] = (own[h] + a_dst[h, t].astype(F32)).astype(BF16)
            b_copy(h, t).start()
        mine(3)
        a_copy(h, 3).wait_recv()
        own[h] = own[h] + a_dst[h, 3].astype(F32)
        return carry

    lax.fori_loop(0, CUTS, gradient, 0)

    def drain_b():
        for h in range(CUTS):
            await_out(a_src.at[h], a_send.at[0])
            await_out(b_src.at[h], b_send.at[0])

    drains.append(drain_b)

    here = y * 4 + f

    def c_copy(h, j):
        to_y, to_f = (y + j // 4) % 4, (f + j % 4) % 4
        other = to_y * 4 + to_f
        return remote(
            c_src.at[h, other],
            c_dst.at[h, here],
            c_send.at[0],
            c_recv.at[h],
            dp=2 * to_y + c,
            vocab=vid(j % 4, 0),
        )

    order_c = (10, 6, 9, 11, 14, 2, 8, 5, 7, 13, 15, 1, 3, 4, 12)
    for h in range(CUTS):
        total = own[h]
        await_in(b_dst.at[h], b_recv.at[h])
        for t in range(3):
            total = total + b_dst[h, t].astype(F32)
        spread = dot_t(selt[...], total.astype(BF16)).astype(BF16)
        c_src[h] = spread.reshape(PEERS, 32, cut)
        for j in order_c:
            c_copy(h, j).start()

    finish()
    stacked = jnp.concatenate([forward, squared, reverse], axis=0)
    share_rows = n_rows // GROUPS
    result = jnp.zeros((3, share_rows), F32)
    for j in range(GROUPS):
        result = jnp.where(group == j, stacked[:, j * share_rows : (j + 1) * share_rows], result)
    out[4:7, 0:share_rows] = result

    for h in range(CUTS):
        c_dst[h, here] = c_src[h, here]
        await_in(c_dst.at[h, pl.ds(0, PEERS - 1)], c_recv.at[h])
        value = c_dst[h, 0].astype(F32)
        for k in range(1, PEERS):
            value = value + c_dst[h, k].astype(F32)
        d_src[:, h * cut : (h + 1) * cut] = value

    def drain_c():
        for h in range(CUTS):
            await_out(c_src.at[h, pl.ds(0, PEERS - 1)], c_send.at[0])

    drains.append(drain_c)

    def d_copy(dc, ds):
        to_c, to_s = (c + dc) % 2, (s + ds) % 4
        at = pl.multiple_of(to_c * 16 + to_s // 2 * 8, 8)
        return remote(
            d_src.at[pl.ds(at, 8)],
            d_dst.at[c * 4 + s],
            d_send.at[0],
            d_recv.at[0],
            dp=2 * y + to_c,
            vocab=vid(0, ds),
        )

    others = [(dc, ds) for ds in (2, 1, 3, 0) for dc in (0, 1) if (dc, ds) != (0, 0)]
    for dc, ds in others:
        d_copy(dc, ds).start()
    finish()
    d_dst[c * 4 + s] = d_src[pl.ds(pl.multiple_of(c * 16 + s // 2 * 8, 8), 8), :]
    await_in(d_dst.at[pl.ds(0, GROUPS - 1)], d_recv.at[0])
    for u in range(GROUPS):
        odd = (z, x)[u // 4] % 2 == 1
        out[0:4, u * chunk : (u + 1) * chunk] = jnp.where(
            odd, d_dst[u, 4:8, :], d_dst[u, 0:4, :]
        )

    def drain_d():
        await_out(d_dst.at[pl.ds(0, GROUPS - 1)], d_send.at[0])

    drains.append(drain_d)
    finish()


def split(both, div_out, grad_out):
    div_out[...] = both[4:7, 0 : div_out.shape[1]]
    grad_out[...] = both[0:4, :]


def body(pol_hidden, ref_hidden, pol_head, ref_head, kept, send_counts, lengths):
    per_group, width = pol_hidden.shape
    shard = pol_head.shape[1]
    n_rows = GROUPS * per_group // 2
    part = width // (4 * PIECES)
    chunk = width // 8
    cut = chunk // CUTS
    vmem = pl.BlockSpec(memory_space=pltpu.VMEM)
    hbm = pl.BlockSpec(memory_space=pl.ANY)
    dma = pltpu.SemaphoreType.DMA
    both = pl.pallas_call(
        kernel,
        out_shape=jax.ShapeDtypeStruct((8, width), F32),
        in_specs=[hbm, hbm, hbm, hbm, vmem, vmem, vmem],
        out_specs=vmem,
        scratch_shapes=[
            pltpu.VMEM((2, width, shard), BF16),
            pltpu.VMEM((PIECES, GROUPS, per_group, part), BF16),
            pltpu.VMEM((2, 4 * PIECES, n_rows, part), BF16),
            pltpu.VMEM((2, n_rows, shard), F32),
            pltpu.VMEM((2, shard, n_rows), F32),
            pltpu.VMEM((shard, n_rows), BF16),
            pltpu.VMEM((GROUPS, 8, 128), jnp.int32),
            pltpu.VMEM((n_rows, 2 * n_rows), BF16),
            pltpu.VMEM((2 * n_rows, n_rows), BF16),
            pltpu.VMEM((8, n_rows), F32),
            pltpu.VMEM((PEERS, 8, n_rows), F32),
            pltpu.VMEM((GROUPS, 8, n_rows), F32),
            pltpu.VMEM((CUTS, 4, cut, n_rows), BF16),
            pltpu.VMEM((CUTS, 4, cut, n_rows), BF16),
            pltpu.VMEM((CUTS, cut, n_rows), F32),
            pltpu.VMEM((CUTS, 3, cut, n_rows), BF16),
            pltpu.VMEM((CUTS, 3, cut, n_rows), BF16),
            pltpu.VMEM((CUTS, PEERS, 32, cut), BF16),
            pltpu.VMEM((CUTS, PEERS, 32, cut), BF16),
            pltpu.VMEM((32, chunk), F32),
            pltpu.VMEM((GROUPS, 8, chunk), F32),
            dma((1,)),
            dma((1,)),
            dma((PIECES,)),
            dma((1,)),
            dma((1,)),
            dma((1,)),
            dma((PIECES,)),
            dma((1,)),
            dma((PIECES // 2,)),
            pltpu.SemaphoreType.REGULAR,
            dma((1,)),
            dma((1,)),
            dma((1,)),
            dma((1,)),
            dma((1,)),
            dma((CUTS, 4)),
            dma((1,)),
            dma((CUTS,)),
            dma((1,)),
            dma((CUTS,)),
            dma((1,)),
            dma((1,)),
        ],
        compiler_params=pltpu.CompilerParams(
            collective_id=0, has_side_effects=True, vmem_limit_bytes=56 * 1024 * 1024
        ),
        cost_estimate=pl.CostEstimate(
            flops=6 * n_rows * width * shard, bytes_accessed=4 * width * shard, transcendentals=0
        ),
        name="divergence_heads",
    )(
        pol_hidden,
        ref_hidden,
        pol_head,
        ref_head,
        kept.reshape(1, per_group),
        send_counts,
        lengths.reshape(1, 2),
    )
    return pl.pallas_call(
        split,
        out_shape=(
            jax.ShapeDtypeStruct((3, n_rows // GROUPS), F32),
            jax.ShapeDtypeStruct((4, width), F32),
        ),
        in_specs=[vmem],
        out_specs=(vmem, vmem),
        name="split_outputs",
    )(both)


def solution(mesh):
    return jax.shard_map(
        body,
        mesh=mesh,
        in_specs=(
            P("dp", None),
            P("dp", None),
            P(None, ("dp", "vocab")),
            P(None, ("dp", "vocab")),
            P("dp"),
            P("dp", None),
            P("dp"),
        ),
        out_specs=(P(None, "dp"), P(("dp", "vocab"), None)),
        check_vma=False,
    )
```

```python
import functools

import jax
import jax.numpy as jnp
from jax import lax
from jax.experimental import pallas as pl
from jax.experimental.pallas import tpu as pltpu
from jax.sharding import PartitionSpec as P

MESH = pl.DeviceIdType.MESH
GROUPS = 8
PEERS = 16
SPAN = 32
PIECES = 8
CUTS = 2
LAG = 3
WIDE = 1
FETCHED = PIECES + 3 * WIDE
POSTED = 6
F32 = jnp.float32
BF16 = jnp.bfloat16


def dot(a, b):
    return lax.dot_general(a, b, (((1,), (0,)), ((), ())), preferred_element_type=F32)


def dot_t(a, b):
    return lax.dot_general(a, b, (((1,), (1,)), ((), ())), preferred_element_type=F32)


def iota(shape, axis):
    return lax.broadcasted_iota(jnp.int32, shape, axis)


def merge_stats(block):
    top_p, top_r = block[:, 0, :], block[:, 1, :]
    s0, s1, s2 = block[:, 2, :], block[:, 3, :], block[:, 4, :]
    r0, r1 = block[:, 5, :], block[:, 6, :]
    best_p = jnp.max(top_p, axis=0, keepdims=True)
    best_r = jnp.max(top_r, axis=0, keepdims=True)
    low_p, low_r = top_p - best_p, top_r - best_r
    shift = low_p - low_r
    scale_p, scale_r = jnp.exp(low_p), jnp.exp(low_r)

    def total(value):
        return jnp.sum(value, axis=0, keepdims=True)

    return (
        best_p,
        best_r,
        total(scale_p * s0),
        total(scale_p * (s1 + shift * s0)),
        total(scale_p * (s2 + shift * (2.0 * s1 + shift * s0))),
        total(scale_r * r0),
        total(scale_r * (r1 + shift * r0)),
    )


def kernel(
    pol_hidden,
    ref_hidden,
    pol_head,
    ref_head,
    kept,
    counts,
    lengths,
    out,
    head,
    gath,
    rows,
    acc,
    logt,
    slope,
    info,
    sel,
    selt,
    length_row,
    stat_v,
    stat_d,
    a_src,
    a_dst,
    own,
    b_src,
    b_dst,
    c_src,
    c_dst,
    d_src,
    d_dst,
    head_sem,
    p1_send,
    p1_recv,
    info_send,
    info_recv,
    ring_send,
    ring_recv,
    sib_send,
    sib_recv,
    token,
    sv_send,
    sv_recv,
    sd_send,
    sd_recv,
    a_send,
    a_recv,
    b_send,
    b_recv,
    c_send,
    c_recv,
    d_send,
    d_recv,
):
    group = lax.axis_index("dp")
    v = lax.axis_index("vocab")
    y, c = group // 2, group % 2
    z, x = v // 4, v % 4
    f = x * (1 - c) + z * c
    s = z * (1 - c) + x * c
    per_group, width = pol_hidden.shape
    part = width // (4 * PIECES)
    half = width // 2
    shard = pol_head.shape[1]
    n_rows = rows.shape[2]

    def vid(df, ds):
        ff, ss = (f + df) % 4, (s + ds) % 4
        return ff * (1 + 3 * c) + ss * (4 - 3 * c)

    def remote(src, dst, send, recv, dp=None, vocab=None):
        target = {}
        if dp is not None:
            target["dp"] = dp
        if vocab is not None:
            target["vocab"] = vocab
        return pltpu.make_async_remote_copy(
            src_ref=src,
            dst_ref=dst,
            send_sem=send,
            recv_sem=recv,
            device_id=target,
            device_id_type=MESH,
        )

    sibling = group + 1 - 2 * c

    def await_in(like, sem):
        remote(like, like, sem, sem, dp=sibling).wait_recv()

    def await_out(like, sem):
        remote(like, like, sem, sem, dp=sibling).wait_send()

    drains = []

    def finish():
        while drains:
            drains.pop(0)()


    quarter = width // 4
    for m, source in enumerate((pol_head, ref_head)):
        for q in range(4):
            at = pl.ds(q * quarter, quarter)
            pltpu.make_async_copy(source.at[at], head.at[m, at], head_sem.at[0]).start()
    barrier = pltpu.get_barrier_semaphore()
    for j in range(1, GROUPS):
        pl.semaphore_signal(
            barrier, inc=1, device_id={"dp": (group + j) % GROUPS}, device_id_type=MESH
        )
    for ds in (1, 2, 3):
        pl.semaphore_signal(
            barrier, inc=1, device_id={"vocab": vid(0, ds)}, device_id_type=MESH
        )
    info[group] = jnp.zeros(info.shape[1:], jnp.int32)
    info[group, 0:1, 0:per_group] = kept[...]
    info[group, 1:2, 0:GROUPS] = counts[...]
    info[group, 2:3, 0:2] = lengths[...]
    pl.semaphore_wait(barrier, GROUPS + 2)

    for j in range(1, GROUPS):
        remote(
            info.at[group],
            info.at[group],
            info_send.at[0],
            info_recv.at[0],
            dp=(group + j) % GROUPS,
        ).start()
    hiddens = (pol_hidden, ref_hidden)

    def fetched(q, quarter):
        extra = jnp.maximum(q - PIECES + WIDE, 0)
        piece = jnp.where(q < PIECES - WIDE, q, PIECES - WIDE + extra // 4)
        return (quarter + extra % 4) % 4 * PIECES + piece

    def part_source(m, q):
        at = pl.multiple_of(fetched(q, (z, x)[m]) * part, part)
        return hiddens[m].at[:, pl.ds(at, part)]

    def part_copy(m, dy, q):
        return remote(
            part_source(m, q),
            gath.at[q, group],
            p1_send.at[0],
            p1_recv.at[q],
            dp=2 * ((y + dy) % 4) + m,
        )

    def local_copy(m, q):
        return pltpu.make_async_copy(part_source(m, q), gath.at[q, group], p1_recv.at[q])

    def each_part(q, act):
        for dy in (2, 1, 3):
            for m in (0, 1):
                act(part_copy(m, dy, q))
        for m in (0, 1):

            @pl.when(c != m)
            def _():
                act(part_copy(m, 0, q))

    def start_parts(q):
        each_part(q, lambda copy: copy.start())
        for m in (0, 1):

            @pl.when(c == m)
            def _():
                local_copy(m, q).start()

    for q in range(POSTED):
        start_parts(q)

    acc[...] = jnp.zeros(acc.shape, F32)

    def drain_parts():
        await_out(info.at[pl.ds(0, GROUPS - 1)], info_send.at[0])
        for q in range(FETCHED):
            await_out(gath.at[q, pl.ds(0, GROUPS - 1)], p1_send.at[0])

    drains.append(drain_parts)

    await_in(info.at[pl.ds(0, GROUPS - 1)], info_recv.at[0])
    kept_g = jnp.concatenate([info[i, 0:1, :] for i in range(GROUPS)], axis=0).astype(F32)
    count_g = jnp.concatenate([info[i, 1:2, :] for i in range(GROUPS)], axis=0).astype(F32)
    length_g = jnp.concatenate([info[i, 2:3, :] for i in range(GROUPS)], axis=0).astype(F32)
    upper = (iota((128, 128), 0) < iota((128, 128), 1)).astype(F32)
    rank = dot(kept_g, upper)
    start = dot(count_g, upper)
    line = jnp.zeros((1, 128), F32)
    lines = []
    for i in range(GROUPS):
        lines.append(line)
        line = line + count_g[i : i + 1, :]
    offset = jnp.concatenate(lines, axis=0)
    placed = jnp.zeros((GROUPS, 128), F32)
    for j in range(GROUPS):
        first = start[:, j : j + 1]
        last = first + count_g[:, j : j + 1]
        target = float(j * (n_rows // GROUPS)) + offset[:, j : j + 1] + rank - first
        placed = placed + jnp.where((first <= rank) & (rank < last), target, 0.0)
    placed = jnp.where(kept_g > 0.5, placed, -1.0)
    lane = iota((GROUPS, 128), 1)
    length_g = jnp.where(lane < SPAN, length_g[:, 0:1], length_g[:, 1:2])
    length_g = jnp.where(kept_g > 0.5, length_g, 0.0)
    placed_r = pltpu.roll(placed, 64, 1)
    length_r = pltpu.roll(length_g, 64, 1)
    place = iota((n_rows, 128), 0).astype(F32)
    low = lane[0:1] < 64
    weight_len = jnp.zeros((8, n_rows), F32)
    for k in range(4):
        pair = jnp.where(low, placed[2 * k : 2 * k + 1], placed_r[2 * k + 1 : 2 * k + 2])
        spans = jnp.where(low, length_g[2 * k : 2 * k + 1], length_r[2 * k + 1 : 2 * k + 2])
        chosen = (place == pair).astype(F32)
        sel[:, k * 128 : (k + 1) * 128] = chosen.astype(BF16)
        weight_len = weight_len + dot_t(jnp.broadcast_to(spans, (8, 128)), chosen)
    length_row[...] = weight_len

    line = iota((2 * n_rows, 2 * n_rows), 0)
    to_f, to_c, to_s = line // 32 % 4, line // 16 % 2, line // 4 % 4
    to_v = to_f * (1 + 3 * c) + to_s * (4 - 3 * c)
    origin = (line // 128 * 2 + to_c) * per_group + to_v * 4 + line % 4
    moved = (iota((2 * n_rows, 2 * n_rows), 1) == origin).astype(F32).astype(BF16)
    selt[...] = dot_t(moved, sel[...]).astype(BF16)
    pltpu.make_async_copy(head, head, head_sem.at[0]).wait()

    def push(slot, q, j):
        return remote(
            rows.at[c, slot],
            rows.at[c, slot],
            ring_send.at[0],
            ring_recv.at[q],
            vocab=vid(0, (1, 3, 2)[j]),
        )

    def share(model, slot):
        return remote(
            rows.at[model, slot],
            rows.at[model, slot],
            sib_send.at[0],
            sib_recv.at[slot % PIECES // 2],
            dp=sibling,
        )

    def order(j):
        return jnp.where(j == 1, 1, jnp.where(j == 2, 3, jnp.where(j == 3, 2, 0)))

    def multiply(model, first, q):
        total = acc[model]
        for k in range(4):
            slot = ((first + k) % 4) * PIECES + 2 * q
            at = pl.ds(pl.multiple_of(slot * part, 2 * part), 2 * part)
            both = jnp.concatenate([rows[model, slot], rows[model, slot + 1]], axis=1)
            total = total + dot(both, head[model, at, :])
        acc[model] = total

    def parts_step(p, carry):
        @pl.when(p < FETCHED)
        def _():
            await_in(gath.at[p], p1_recv.at[p])
            slot = fetched(p, s)
            packed = gath[p].reshape(GROUPS * per_group, part)
            rows[c, slot] = dot(sel[...], packed).astype(BF16)

            @pl.when(p < PIECES - WIDE)
            def _():
                for j in range(3):
                    push(slot, p, j).start()

            share(c, slot).start()

            @pl.when(p < FETCHED - POSTED)
            def _():
                start_parts(p + POSTED)


        def side(i, carry):
            t = p - LAG - 1 + i
            mine = i == 1
            first = jnp.where(mine, s, f)
            model = jnp.where(mine, c, 1 - c)

            @pl.when((t >= 0) & (t < PIECES))
            def _():
                @pl.when(mine & (t < PIECES - WIDE))
                def _():
                    await_in(rows.at[c, pl.ds(0, 3)], ring_recv.at[t])
                    for j in range(3):
                        share(c, (s + 1 + j) % 4 * PIECES + t).start()

                @pl.when(t % 2 == 1)
                def _():
                    @pl.when(i == 0)
                    def _():
                        await_in(rows.at[1 - c, pl.ds(0, 8)], sib_recv.at[t // 2])

                    multiply(model, first, t // 2)

            return carry

        lax.fori_loop(0, 2, side, 0)
        return carry

    lax.fori_loop(0, PIECES + LAG + 1, parts_step, 0)

    def drain_ring():
        await_out(rows.at[0, pl.ds(0, 3 * (PIECES - WIDE))], ring_send.at[0])
        await_out(rows.at[0], sib_send.at[0])

    drains.append(drain_ring)

    chunks = shard // 128
    for m in (0, 1):
        for q in range(chunks):
            at = slice(q * 128, (q + 1) * 128)
            logt[m, at, :] = jnp.transpose(acc[m, :, at])
    top_p = jnp.max(logt[0], axis=0, keepdims=True)
    top_r = jnp.max(logt[1], axis=0, keepdims=True)
    step = 32
    zero = jnp.zeros((8, n_rows), F32)

    def fold(value):
        return jnp.sum(value.reshape(step // 8, 8, n_rows), axis=0)

    def local_sums(q, carry):
        s0, s1, s2, r0, r1 = carry
        at = pl.ds(pl.multiple_of(q * step, step), step)
        lp = logt[0, at, :] - top_p
        lr = logt[1, at, :] - top_r
        ep, er = jnp.exp(lp), jnp.exp(lr)
        d = lp - lr
        ed = ep * d
        return (
            s0 + fold(ep),
            s1 + fold(ed),
            s2 + fold(ed * d),
            r0 + fold(er),
            r1 + fold(er * d),
        )

    sums = lax.fori_loop(0, shard // step, local_sums, (zero,) * 5)
    sums = [jnp.sum(value, axis=0, keepdims=True) for value in sums]
    blank = jnp.zeros((1, n_rows), F32)
    stat_d[group] = jnp.concatenate([top_p, top_r, *sums, blank], axis=0)
    for j in range(1, GROUPS):
        remote(
            stat_d.at[group],
            stat_d.at[group],
            sd_send.at[0],
            sd_recv.at[0],
            dp=(group + j) % GROUPS,
        ).start()
    for ds in (1, 2, 3):
        pl.semaphore_signal(token, inc=1, device_id={"vocab": vid(0, ds)}, device_id_type=MESH)
    await_in(stat_d.at[pl.ds(0, GROUPS - 1)], sd_recv.at[0])
    pl.semaphore_wait(token, 3)

    def drain_stat_d():
        await_out(stat_d.at[pl.ds(0, GROUPS - 1)], sd_send.at[0])

    drains.append(drain_stat_d)
    stat_v[v] = jnp.concatenate([*merge_stats(stat_d), blank], axis=0)
    for j in range(1, PEERS):
        remote(
            stat_v.at[v], stat_v.at[v], sv_send.at[0], sv_recv.at[0], vocab=(v + j) % PEERS
        ).start()
    finish()
    await_in(stat_v.at[pl.ds(0, PEERS - 1)], sv_recv.at[0])

    def drain_stat_v():
        await_out(stat_v.at[pl.ds(0, PEERS - 1)], sv_send.at[0])

    drains.append(drain_stat_v)
    top_p, top_r, s0, s1, s2, r0, r1 = merge_stats(stat_v)
    log_s, log_r = jnp.log(s0), jnp.log(r0)
    norm_p, norm_r = top_p + log_s, top_r + log_r
    move = log_r - log_s
    forward = s1 / s0 + move
    squared = 0.5 * ((s2 + move * (2.0 * s1)) / s0 + move * move)
    reverse = -(r1 / r0 + move)
    both = forward + squared
    weight = float(SPAN) / length_row[0:1, :]

    def slopes(q, carry):
        at = pl.ds(pl.multiple_of(q * step, step), step)
        lp = logt[0, at, :] - norm_p
        d = lp - (logt[1, at, :] - norm_r)
        slope[at, :] = (weight * jnp.exp(lp) * (0.5 * d * d + d - both)).astype(BF16)
        return carry

    lax.fori_loop(0, shard // step, slopes, 0)

    chunk = half // 4
    order_s = (2, 1, 3, 0)

    cut = chunk // CUTS

    def start_of(core, index, h):
        return pl.multiple_of(core * half + index * chunk + h * cut, cut)

    def a_copy(h, t):
        return remote(
            a_src.at[h, t], a_dst.at[h, t], a_send.at[0], a_recv.at[h, t], dp=sibling
        )

    def b_copy(h, t):
        return remote(
            b_src.at[h, t],
            b_dst.at[h, t],
            b_send.at[0],
            b_recv.at[h],
            vocab=vid(0, order_s[t]),
        )

    def gradient(h, carry):
        def theirs(t):
            at = start_of(1 - c, (f + order_s[t]) % 4, h)
            a_src[h, t] = dot(head[0, pl.ds(at, cut), :], slope[...]).astype(BF16)
            a_copy(h, t).start()

        def mine(t):
            at = start_of(c, (s + order_s[t]) % 4, h)
            own[h] = dot(head[0, pl.ds(at, cut), :], slope[...])

        theirs(0)
        theirs(1)
        for t in range(3):
            mine(t)
            if t < 2:
                theirs(t + 2)
            a_copy(h, t).wait_recv()
            b_src[h, t] = (own[h] + a_dst[h, t].astype(F32)).astype(BF16)
            b_copy(h, t).start()
        mine(3)
        a_copy(h, 3).wait_recv()
        own[h] = own[h] + a_dst[h, 3].astype(F32)
        return carry

    lax.fori_loop(0, CUTS, gradient, 0)

    def drain_b():
        for h in range(CUTS):
            await_out(a_src.at[h], a_send.at[0])
            await_out(b_src.at[h], b_send.at[0])

    drains.append(drain_b)

    here = y * 4 + f

    def c_copy(h, j):
        to_y, to_f = (y + j // 4) % 4, (f + j % 4) % 4
        other = to_y * 4 + to_f
        return remote(
            c_src.at[h, other],
            c_dst.at[h, here],
            c_send.at[0],
            c_recv.at[h],
            dp=2 * to_y + c,
            vocab=vid(j % 4, 0),
        )

    order_c = (10, 6, 9, 11, 14, 2, 8, 5, 7, 13, 15, 1, 3, 4, 12)
    for h in range(CUTS):
        total = own[h]
        await_in(b_dst.at[h], b_recv.at[h])
        for t in range(3):
            total = total + b_dst[h, t].astype(F32)
        spread = dot_t(selt[...], total.astype(BF16)).astype(BF16)
        c_src[h] = spread.reshape(PEERS, 32, cut)
        for j in order_c:
            c_copy(h, j).start()

    finish()
    stacked = jnp.concatenate([forward, squared, reverse], axis=0)
    share_rows = n_rows // GROUPS
    result = jnp.zeros((3, share_rows), F32)
    for j in range(GROUPS):
        result = jnp.where(group == j, stacked[:, j * share_rows : (j + 1) * share_rows], result)
    out[4:7, 0:share_rows] = result

    for h in range(CUTS):
        c_dst[h, here] = c_src[h, here]
        await_in(c_dst.at[h, pl.ds(0, PEERS - 1)], c_recv.at[h])
        value = c_dst[h, 0].astype(F32)
        for k in range(1, PEERS):
            value = value + c_dst[h, k].astype(F32)
        d_src[:, h * cut : (h + 1) * cut] = value

    def drain_c():
        for h in range(CUTS):
            await_out(c_src.at[h, pl.ds(0, PEERS - 1)], c_send.at[0])

    drains.append(drain_c)

    def d_copy(dc, ds):
        to_c, to_s = (c + dc) % 2, (s + ds) % 4
        at = pl.multiple_of(to_c * 16 + to_s // 2 * 8, 8)
        return remote(
            d_src.at[pl.ds(at, 8)],
            d_dst.at[c * 4 + s],
            d_send.at[0],
            d_recv.at[0],
            dp=2 * y + to_c,
            vocab=vid(0, ds),
        )

    others = [(dc, ds) for ds in (2, 1, 3, 0) for dc in (0, 1) if (dc, ds) != (0, 0)]
    for dc, ds in others:
        d_copy(dc, ds).start()
    finish()
    d_dst[c * 4 + s] = d_src[pl.ds(pl.multiple_of(c * 16 + s // 2 * 8, 8), 8), :]
    await_in(d_dst.at[pl.ds(0, GROUPS - 1)], d_recv.at[0])
    for u in range(GROUPS):
        odd = (z, x)[u // 4] % 2 == 1
        out[0:4, u * chunk : (u + 1) * chunk] = jnp.where(
            odd, d_dst[u, 4:8, :], d_dst[u, 0:4, :]
        )

    def drain_d():
        await_out(d_dst.at[pl.ds(0, GROUPS - 1)], d_send.at[0])

    drains.append(drain_d)
    finish()


def split(both, div_out, grad_out):
    div_out[...] = both[4:7, 0 : div_out.shape[1]]
    grad_out[...] = both[0:4, :]


def body(pol_hidden, ref_hidden, pol_head, ref_head, kept, send_counts, lengths):
    per_group, width = pol_hidden.shape
    shard = pol_head.shape[1]
    n_rows = GROUPS * per_group // 2
    part = width // (4 * PIECES)
    chunk = width // 8
    cut = chunk // CUTS
    vmem = pl.BlockSpec(memory_space=pltpu.VMEM)
    hbm = pl.BlockSpec(memory_space=pl.ANY)
    dma = pltpu.SemaphoreType.DMA
    both = pl.pallas_call(
        kernel,
        out_shape=jax.ShapeDtypeStruct((8, width), F32),
        in_specs=[hbm, hbm, hbm, hbm, vmem, vmem, vmem],
        out_specs=vmem,
        scratch_shapes=[
            pltpu.VMEM((2, width, shard), BF16),
            pltpu.VMEM((FETCHED, GROUPS, per_group, part), BF16),
            pltpu.VMEM((2, 4 * PIECES, n_rows, part), BF16),
            pltpu.VMEM((2, n_rows, shard), F32),
            pltpu.VMEM((2, shard, n_rows), F32),
            pltpu.VMEM((shard, n_rows), BF16),
            pltpu.VMEM((GROUPS, 8, 128), jnp.int32),
            pltpu.VMEM((n_rows, 2 * n_rows), BF16),
            pltpu.VMEM((2 * n_rows, n_rows), BF16),
            pltpu.VMEM((8, n_rows), F32),
            pltpu.VMEM((PEERS, 8, n_rows), F32),
            pltpu.VMEM((GROUPS, 8, n_rows), F32),
            pltpu.VMEM((CUTS, 4, cut, n_rows), BF16),
            pltpu.VMEM((CUTS, 4, cut, n_rows), BF16),
            pltpu.VMEM((CUTS, cut, n_rows), F32),
            pltpu.VMEM((CUTS, 3, cut, n_rows), BF16),
            pltpu.VMEM((CUTS, 3, cut, n_rows), BF16),
            pltpu.VMEM((CUTS, PEERS, 32, cut), BF16),
            pltpu.VMEM((CUTS, PEERS, 32, cut), BF16),
            pltpu.VMEM((32, chunk), F32),
            pltpu.VMEM((GROUPS, 8, chunk), F32),
            dma((1,)),
            dma((1,)),
            dma((FETCHED,)),
            dma((1,)),
            dma((1,)),
            dma((1,)),
            dma((PIECES,)),
            dma((1,)),
            dma((PIECES // 2,)),
            pltpu.SemaphoreType.REGULAR,
            dma((1,)),
            dma((1,)),
            dma((1,)),
            dma((1,)),
            dma((1,)),
            dma((CUTS, 4)),
            dma((1,)),
            dma((CUTS,)),
            dma((1,)),
            dma((CUTS,)),
            dma((1,)),
            dma((1,)),
        ],
        compiler_params=pltpu.CompilerParams(
            collective_id=0, has_side_effects=True, vmem_limit_bytes=56 * 1024 * 1024
        ),
        cost_estimate=pl.CostEstimate(
            flops=6 * n_rows * width * shard, bytes_accessed=4 * width * shard, transcendentals=0
        ),
        name="divergence_heads",
    )(
        pol_hidden,
        ref_hidden,
        pol_head,
        ref_head,
        kept.reshape(1, per_group),
        send_counts,
        lengths.reshape(1, 2),
    )
    return pl.pallas_call(
        split,
        out_shape=(
            jax.ShapeDtypeStruct((3, n_rows // GROUPS), F32),
            jax.ShapeDtypeStruct((4, width), F32),
        ),
        in_specs=[vmem],
        out_specs=(vmem, vmem),
        name="split_outputs",
    )(both)


def solution(mesh):
    return jax.shard_map(
        body,
        mesh=mesh,
        in_specs=(
            P("dp", None),
            P("dp", None),
            P(None, ("dp", "vocab")),
            P(None, ("dp", "vocab")),
            P("dp"),
            P("dp", None),
            P("dp"),
        ),
        out_specs=(P(None, "dp"), P(("dp", "vocab"), None)),
        check_vma=False,
    )
```

```python
import functools

import jax
import jax.numpy as jnp
from jax import lax
from jax.experimental import pallas as pl
from jax.experimental.pallas import tpu as pltpu
from jax.sharding import PartitionSpec as P

MESH = pl.DeviceIdType.MESH
GROUPS = 8
PEERS = 16
SPAN = 32
PIECES = 8
CUTS = 2
LAG = 3
WIDE = 1
FETCHED = PIECES + 3 * WIDE
POSTED = 6
F32 = jnp.float32
BF16 = jnp.bfloat16


def dot(a, b):
    return lax.dot_general(a, b, (((1,), (0,)), ((), ())), preferred_element_type=F32)


def dot_t(a, b):
    return lax.dot_general(a, b, (((1,), (1,)), ((), ())), preferred_element_type=F32)


def iota(shape, axis):
    return lax.broadcasted_iota(jnp.int32, shape, axis)


def merge_stats(block):
    top_p, top_r = block[:, 0, :], block[:, 1, :]
    s0, s1, s2 = block[:, 2, :], block[:, 3, :], block[:, 4, :]
    r0, r1 = block[:, 5, :], block[:, 6, :]
    best_p = jnp.max(top_p, axis=0, keepdims=True)
    best_r = jnp.max(top_r, axis=0, keepdims=True)
    low_p, low_r = top_p - best_p, top_r - best_r
    shift = low_p - low_r
    scale_p, scale_r = jnp.exp(low_p), jnp.exp(low_r)

    def total(value):
        return jnp.sum(value, axis=0, keepdims=True)

    return (
        best_p,
        best_r,
        total(scale_p * s0),
        total(scale_p * (s1 + shift * s0)),
        total(scale_p * (s2 + shift * (2.0 * s1 + shift * s0))),
        total(scale_r * r0),
        total(scale_r * (r1 + shift * r0)),
    )


def kernel(
    pol_hidden,
    ref_hidden,
    pol_head,
    ref_head,
    kept,
    counts,
    lengths,
    out,
    head,
    gath,
    rows,
    acc,
    logt,
    slope,
    info,
    sel,
    selt,
    length_row,
    stat_v,
    stat_d,
    a_src,
    a_dst,
    own,
    b_src,
    b_dst,
    c_src,
    c_dst,
    d_src,
    d_dst,
    head_sem,
    p1_send,
    p1_recv,
    info_send,
    info_recv,
    ring_send,
    ring_recv,
    sib_send,
    sib_recv,
    token,
    sv_send,
    sv_recv,
    sd_send,
    sd_recv,
    a_send,
    a_recv,
    b_send,
    b_recv,
    c_send,
    c_recv,
    d_send,
    d_recv,
):
    group = lax.axis_index("dp")
    v = lax.axis_index("vocab")
    y, c = group // 2, group % 2
    z, x = v // 4, v % 4
    f = x * (1 - c) + z * c
    s = z * (1 - c) + x * c
    per_group, width = pol_hidden.shape
    part = width // (4 * PIECES)
    half = width // 2
    shard = pol_head.shape[1]
    n_rows = rows.shape[2]

    def vid(df, ds):
        ff, ss = (f + df) % 4, (s + ds) % 4
        return ff * (1 + 3 * c) + ss * (4 - 3 * c)

    def remote(src, dst, send, recv, dp=None, vocab=None):
        target = {}
        if dp is not None:
            target["dp"] = dp
        if vocab is not None:
            target["vocab"] = vocab
        return pltpu.make_async_remote_copy(
            src_ref=src,
            dst_ref=dst,
            send_sem=send,
            recv_sem=recv,
            device_id=target,
            device_id_type=MESH,
        )

    sibling = group + 1 - 2 * c

    def await_in(like, sem):
        remote(like, like, sem, sem, dp=sibling).wait_recv()

    def await_out(like, sem):
        remote(like, like, sem, sem, dp=sibling).wait_send()

    drains = []

    def finish():
        while drains:
            drains.pop(0)()


    quarter = width // 4
    for m, source in enumerate((pol_head, ref_head)):
        for q in range(4):
            at = pl.ds(q * quarter, quarter)
            pltpu.make_async_copy(source.at[at], head.at[m, at], head_sem.at[0]).start()
    barrier = pltpu.get_barrier_semaphore()
    for j in range(1, GROUPS):
        pl.semaphore_signal(
            barrier, inc=1, device_id={"dp": (group + j) % GROUPS}, device_id_type=MESH
        )
    for ds in (1, 2, 3):
        pl.semaphore_signal(
            barrier, inc=1, device_id={"vocab": vid(0, ds)}, device_id_type=MESH
        )
    info[group] = jnp.zeros(info.shape[1:], jnp.int32)
    info[group, 0:1, 0:per_group] = kept[...]
    info[group, 1:2, 0:GROUPS] = counts[...]
    info[group, 2:3, 0:2] = lengths[...]
    acc[...] = jnp.zeros(acc.shape, F32)
    pl.semaphore_wait(barrier, GROUPS + 2)

    for j in range(1, GROUPS):
        remote(
            info.at[group],
            info.at[group],
            info_send.at[0],
            info_recv.at[0],
            dp=(group + j) % GROUPS,
        ).start()
    hiddens = (pol_hidden, ref_hidden)

    def fetched(q, quarter):
        extra = jnp.maximum(q - PIECES + WIDE, 0)
        piece = jnp.where(q < PIECES - WIDE, q, PIECES - WIDE + extra // 4)
        return (quarter + extra % 4) % 4 * PIECES + piece

    def part_source(m, q):
        at = pl.multiple_of(fetched(q, (z, x)[m]) * part, part)
        return hiddens[m].at[:, pl.ds(at, part)]

    def part_copy(m, dy, q):
        return remote(
            part_source(m, q),
            gath.at[q, group],
            p1_send.at[0],
            p1_recv.at[q],
            dp=2 * ((y + dy) % 4) + m,
        )

    def local_copy(m, q):
        return pltpu.make_async_copy(part_source(m, q), gath.at[q, group], p1_recv.at[q])

    def each_part(q, act):
        for dy in (2, 1, 3):
            for m in (0, 1):
                act(part_copy(m, dy, q))
        for m in (0, 1):

            @pl.when(c != m)
            def _():
                act(part_copy(m, 0, q))

    def start_parts(q):
        each_part(q, lambda copy: copy.start())
        for m in (0, 1):

            @pl.when(c == m)
            def _():
                local_copy(m, q).start()

    for q in range(POSTED):
        start_parts(q)


    def drain_parts():
        await_out(info.at[pl.ds(0, GROUPS - 1)], info_send.at[0])
        for q in range(FETCHED):
            await_out(gath.at[q, pl.ds(0, GROUPS - 1)], p1_send.at[0])

    drains.append(drain_parts)

    await_in(info.at[pl.ds(0, GROUPS - 1)], info_recv.at[0])
    kept_g = jnp.concatenate([info[i, 0:1, :] for i in range(GROUPS)], axis=0).astype(F32)
    count_g = jnp.concatenate([info[i, 1:2, :] for i in range(GROUPS)], axis=0).astype(F32)
    length_g = jnp.concatenate([info[i, 2:3, :] for i in range(GROUPS)], axis=0).astype(F32)
    upper = (iota((128, 128), 0) < iota((128, 128), 1)).astype(F32)
    rank = dot(kept_g, upper)
    start = dot(count_g, upper)
    line = jnp.zeros((1, 128), F32)
    lines = []
    for i in range(GROUPS):
        lines.append(line)
        line = line + count_g[i : i + 1, :]
    offset = jnp.concatenate(lines, axis=0)
    placed = jnp.zeros((GROUPS, 128), F32)
    for j in range(GROUPS):
        first = start[:, j : j + 1]
        last = first + count_g[:, j : j + 1]
        target = float(j * (n_rows // GROUPS)) + offset[:, j : j + 1] + rank - first
        placed = placed + jnp.where((first <= rank) & (rank < last), target, 0.0)
    placed = jnp.where(kept_g > 0.5, placed, -1.0)
    lane = iota((GROUPS, 128), 1)
    length_g = jnp.where(lane < SPAN, length_g[:, 0:1], length_g[:, 1:2])
    length_g = jnp.where(kept_g > 0.5, length_g, 0.0)
    placed_r = pltpu.roll(placed, 64, 1)
    length_r = pltpu.roll(length_g, 64, 1)
    place = iota((n_rows, 128), 0).astype(F32)
    low = lane[0:1] < 64
    weight_len = jnp.zeros((8, n_rows), F32)
    for k in range(4):
        pair = jnp.where(low, placed[2 * k : 2 * k + 1], placed_r[2 * k + 1 : 2 * k + 2])
        spans = jnp.where(low, length_g[2 * k : 2 * k + 1], length_r[2 * k + 1 : 2 * k + 2])
        chosen = (place == pair).astype(F32)
        sel[:, k * 128 : (k + 1) * 128] = chosen.astype(BF16)
        weight_len = weight_len + dot_t(jnp.broadcast_to(spans, (8, 128)), chosen)
    length_row[...] = weight_len

    line = iota((2 * n_rows, 2 * n_rows), 0)
    to_f, to_c, to_s = line // 32 % 4, line // 16 % 2, line // 4 % 4
    to_v = to_f * (1 + 3 * c) + to_s * (4 - 3 * c)
    origin = (line // 128 * 2 + to_c) * per_group + to_v * 4 + line % 4
    moved = (iota((2 * n_rows, 2 * n_rows), 1) == origin).astype(F32).astype(BF16)
    selt[...] = dot_t(moved, sel[...]).astype(BF16)
    pltpu.make_async_copy(head, head, head_sem.at[0]).wait()

    def push(slot, q, j):
        return remote(
            rows.at[c, slot],
            rows.at[c, slot],
            ring_send.at[0],
            ring_recv.at[q],
            vocab=vid(0, (2, 1, 3)[j]),
        )

    def share(model, slot):
        return remote(
            rows.at[model, slot],
            rows.at[model, slot],
            sib_send.at[0],
            sib_recv.at[slot % PIECES // 2],
            dp=sibling,
        )

    def order(j):
        return jnp.where(j == 1, 1, jnp.where(j == 2, 3, jnp.where(j == 3, 2, 0)))

    def multiply(model, first, q):
        total = acc[model]
        for k in range(4):
            slot = ((first + k) % 4) * PIECES + 2 * q
            at = pl.ds(pl.multiple_of(slot * part, 2 * part), 2 * part)
            both = jnp.concatenate([rows[model, slot], rows[model, slot + 1]], axis=1)
            total = total + dot(both, head[model, at, :])
        acc[model] = total

    def parts_step(p, carry):
        @pl.when(p < FETCHED)
        def _():
            await_in(gath.at[p], p1_recv.at[p])
            slot = fetched(p, s)
            packed = gath[p].reshape(GROUPS * per_group, part)
            rows[c, slot] = dot(sel[...], packed).astype(BF16)

            @pl.when(p < PIECES - WIDE)
            def _():
                for j in range(3):
                    push(slot, p, j).start()

            share(c, slot).start()

            @pl.when(p < FETCHED - POSTED)
            def _():
                start_parts(p + POSTED)


        def side(i, carry):
            t = p - LAG - 1 + i
            mine = i == 1
            first = jnp.where(mine, s, f)
            model = jnp.where(mine, c, 1 - c)

            @pl.when((t >= 0) & (t < PIECES))
            def _():
                @pl.when(mine & (t < PIECES - WIDE))
                def _():
                    await_in(rows.at[c, pl.ds(0, 3)], ring_recv.at[t])
                    for j in range(3):
                        share(c, (s + 1 + j) % 4 * PIECES + t).start()

                @pl.when(t % 2 == 1)
                def _():
                    @pl.when(i == 0)
                    def _():
                        await_in(rows.at[1 - c, pl.ds(0, 8)], sib_recv.at[t // 2])

                    multiply(model, first, t // 2)

            return carry

        lax.fori_loop(0, 2, side, 0)
        return carry

    lax.fori_loop(0, PIECES + LAG + 1, parts_step, 0)

    def drain_ring():
        await_out(rows.at[0, pl.ds(0, 3 * (PIECES - WIDE))], ring_send.at[0])
        await_out(rows.at[0], sib_send.at[0])

    drains.append(drain_ring)

    chunks = shard // 128
    for m in (0, 1):
        for q in range(chunks):
            at = slice(q * 128, (q + 1) * 128)
            logt[m, at, :] = jnp.transpose(acc[m, :, at])
    top_p = jnp.max(logt[0], axis=0, keepdims=True)
    top_r = jnp.max(logt[1], axis=0, keepdims=True)
    step = 32
    zero = jnp.zeros((8, n_rows), F32)

    def fold(value):
        return jnp.sum(value.reshape(step // 8, 8, n_rows), axis=0)

    def local_sums(q, carry):
        s0, s1, s2, r0, r1 = carry
        at = pl.ds(pl.multiple_of(q * step, step), step)
        lp = logt[0, at, :] - top_p
        lr = logt[1, at, :] - top_r
        ep, er = jnp.exp(lp), jnp.exp(lr)
        d = lp - lr
        ed = ep * d
        return (
            s0 + fold(ep),
            s1 + fold(ed),
            s2 + fold(ed * d),
            r0 + fold(er),
            r1 + fold(er * d),
        )

    sums = lax.fori_loop(0, shard // step, local_sums, (zero,) * 5)
    sums = [jnp.sum(value, axis=0, keepdims=True) for value in sums]
    blank = jnp.zeros((1, n_rows), F32)
    stat_d[group] = jnp.concatenate([top_p, top_r, *sums, blank], axis=0)
    for j in range(1, GROUPS):
        remote(
            stat_d.at[group],
            stat_d.at[group],
            sd_send.at[0],
            sd_recv.at[0],
            dp=(group + j) % GROUPS,
        ).start()
    for ds in (1, 2, 3):
        pl.semaphore_signal(token, inc=1, device_id={"vocab": vid(0, ds)}, device_id_type=MESH)
    await_in(stat_d.at[pl.ds(0, GROUPS - 1)], sd_recv.at[0])
    pl.semaphore_wait(token, 3)

    def drain_stat_d():
        await_out(stat_d.at[pl.ds(0, GROUPS - 1)], sd_send.at[0])

    drains.append(drain_stat_d)
    stat_v[v] = jnp.concatenate([*merge_stats(stat_d), blank], axis=0)
    for j in (10, 6, 9, 11, 14, 2, 8, 5, 7, 13, 15, 1, 3, 4, 12):
        remote(
            stat_v.at[v], stat_v.at[v], sv_send.at[0], sv_recv.at[0], vocab=(v + j) % PEERS
        ).start()
    finish()
    await_in(stat_v.at[pl.ds(0, PEERS - 1)], sv_recv.at[0])

    def drain_stat_v():
        await_out(stat_v.at[pl.ds(0, PEERS - 1)], sv_send.at[0])

    drains.append(drain_stat_v)
    top_p, top_r, s0, s1, s2, r0, r1 = merge_stats(stat_v)
    log_s, log_r = jnp.log(s0), jnp.log(r0)
    norm_p, norm_r = top_p + log_s, top_r + log_r
    move = log_r - log_s
    forward = s1 / s0 + move
    squared = 0.5 * ((s2 + move * (2.0 * s1)) / s0 + move * move)
    reverse = -(r1 / r0 + move)
    both = forward + squared
    weight = float(SPAN) / length_row[0:1, :]

    def slopes(q, carry):
        at = pl.ds(pl.multiple_of(q * step, step), step)
        lp = logt[0, at, :] - norm_p
        d = lp - (logt[1, at, :] - norm_r)
        slope[at, :] = (weight * jnp.exp(lp) * (0.5 * d * d + d - both)).astype(BF16)
        return carry

    lax.fori_loop(0, shard // step, slopes, 0)

    chunk = half // 4
    order_s = (2, 1, 3, 0)

    cut = chunk // CUTS

    def start_of(core, index, h):
        return pl.multiple_of(core * half + index * chunk + h * cut, cut)

    def a_copy(h, t):
        return remote(
            a_src.at[h, t], a_dst.at[h, t], a_send.at[0], a_recv.at[h, t], dp=sibling
        )

    def b_copy(h, t):
        return remote(
            b_src.at[h, t],
            b_dst.at[h, t],
            b_send.at[0],
            b_recv.at[h],
            vocab=vid(0, order_s[t]),
        )

    def gradient(h, carry):
        def theirs(t):
            at = start_of(1 - c, (f + order_s[t]) % 4, h)
            a_src[h, t] = dot(head[0, pl.ds(at, cut), :], slope[...]).astype(BF16)
            a_copy(h, t).start()

        def mine(t):
            at = start_of(c, (s + order_s[t]) % 4, h)
            own[h] = dot(head[0, pl.ds(at, cut), :], slope[...])

        theirs(0)
        theirs(1)
        for t in range(3):
            mine(t)
            if t < 2:
                theirs(t + 2)
            a_copy(h, t).wait_recv()
            b_src[h, t] = (own[h] + a_dst[h, t].astype(F32)).astype(BF16)
            b_copy(h, t).start()
        mine(3)
        a_copy(h, 3).wait_recv()
        own[h] = own[h] + a_dst[h, 3].astype(F32)
        return carry

    lax.fori_loop(0, CUTS, gradient, 0)

    def drain_b():
        for h in range(CUTS):
            await_out(a_src.at[h], a_send.at[0])
            await_out(b_src.at[h], b_send.at[0])

    drains.append(drain_b)

    here = y * 4 + f

    def c_copy(h, j):
        to_y, to_f = (y + j // 4) % 4, (f + j % 4) % 4
        other = to_y * 4 + to_f
        return remote(
            c_src.at[h, other],
            c_dst.at[h, here],
            c_send.at[0],
            c_recv.at[h],
            dp=2 * to_y + c,
            vocab=vid(j % 4, 0),
        )

    order_c = (10, 9, 11, 8, 6, 14, 5, 7, 13, 15, 4, 12, 2, 1, 3)
    for h in range(CUTS):
        total = own[h]
        await_in(b_dst.at[h], b_recv.at[h])
        for t in range(3):
            total = total + b_dst[h, t].astype(F32)
        spread = dot_t(selt[...], total.astype(BF16)).astype(BF16)
        c_src[h] = spread.reshape(PEERS, 32, cut)
        for j in order_c:
            c_copy(h, j).start()

    finish()
    stacked = jnp.concatenate([forward, squared, reverse], axis=0)
    share_rows = n_rows // GROUPS
    result = jnp.zeros((3, share_rows), F32)
    for j in range(GROUPS):
        result = jnp.where(group == j, stacked[:, j * share_rows : (j + 1) * share_rows], result)
    out[4:7, 0:share_rows] = result

    for h in range(CUTS):
        c_dst[h, here] = c_src[h, here]
        await_in(c_dst.at[h, pl.ds(0, PEERS - 1)], c_recv.at[h])
        value = c_dst[h, 0].astype(F32)
        for k in range(1, PEERS):
            value = value + c_dst[h, k].astype(F32)
        d_src[:, h * cut : (h + 1) * cut] = value

    def drain_c():
        for h in range(CUTS):
            await_out(c_src.at[h, pl.ds(0, PEERS - 1)], c_send.at[0])

    drains.append(drain_c)

    def d_copy(dc, ds):
        to_c, to_s = (c + dc) % 2, (s + ds) % 4
        at = pl.multiple_of(to_c * 16 + to_s // 2 * 8, 8)
        return remote(
            d_src.at[pl.ds(at, 8)],
            d_dst.at[c * 4 + s],
            d_send.at[0],
            d_recv.at[0],
            dp=2 * y + to_c,
            vocab=vid(0, ds),
        )

    others = [(dc, ds) for ds in (2, 1, 3, 0) for dc in (0, 1) if (dc, ds) != (0, 0)]
    for dc, ds in others:
        d_copy(dc, ds).start()
    finish()
    d_dst[c * 4 + s] = d_src[pl.ds(pl.multiple_of(c * 16 + s // 2 * 8, 8), 8), :]
    await_in(d_dst.at[pl.ds(0, GROUPS - 1)], d_recv.at[0])
    for u in range(GROUPS):
        odd = (z, x)[u // 4] % 2 == 1
        out[0:4, u * chunk : (u + 1) * chunk] = jnp.where(
            odd, d_dst[u, 4:8, :], d_dst[u, 0:4, :]
        )

    def drain_d():
        await_out(d_dst.at[pl.ds(0, GROUPS - 1)], d_send.at[0])

    drains.append(drain_d)
    finish()


def split(both, div_out, grad_out):
    div_out[...] = both[4:7, 0 : div_out.shape[1]]
    grad_out[...] = both[0:4, :]


def body(pol_hidden, ref_hidden, pol_head, ref_head, kept, send_counts, lengths):
    per_group, width = pol_hidden.shape
    shard = pol_head.shape[1]
    n_rows = GROUPS * per_group // 2
    part = width // (4 * PIECES)
    chunk = width // 8
    cut = chunk // CUTS
    vmem = pl.BlockSpec(memory_space=pltpu.VMEM)
    hbm = pl.BlockSpec(memory_space=pl.ANY)
    dma = pltpu.SemaphoreType.DMA
    both = pl.pallas_call(
        kernel,
        out_shape=jax.ShapeDtypeStruct((8, width), F32),
        in_specs=[hbm, hbm, hbm, hbm, vmem, vmem, vmem],
        out_specs=vmem,
        scratch_shapes=[
            pltpu.VMEM((2, width, shard), BF16),
            pltpu.VMEM((FETCHED, GROUPS, per_group, part), BF16),
            pltpu.VMEM((2, 4 * PIECES, n_rows, part), BF16),
            pltpu.VMEM((2, n_rows, shard), F32),
            pltpu.VMEM((2, shard, n_rows), F32),
            pltpu.VMEM((shard, n_rows), BF16),
            pltpu.VMEM((GROUPS, 8, 128), jnp.int32),
            pltpu.VMEM((n_rows, 2 * n_rows), BF16),
            pltpu.VMEM((2 * n_rows, n_rows), BF16),
            pltpu.VMEM((8, n_rows), F32),
            pltpu.VMEM((PEERS, 8, n_rows), F32),
            pltpu.VMEM((GROUPS, 8, n_rows), F32),
            pltpu.VMEM((CUTS, 4, cut, n_rows), BF16),
            pltpu.VMEM((CUTS, 4, cut, n_rows), BF16),
            pltpu.VMEM((CUTS, cut, n_rows), F32),
            pltpu.VMEM((CUTS, 3, cut, n_rows), BF16),
            pltpu.VMEM((CUTS, 3, cut, n_rows), BF16),
            pltpu.VMEM((CUTS, PEERS, 32, cut), BF16),
            pltpu.VMEM((CUTS, PEERS, 32, cut), BF16),
            pltpu.VMEM((32, chunk), F32),
            pltpu.VMEM((GROUPS, 8, chunk), F32),
            dma((1,)),
            dma((1,)),
            dma((FETCHED,)),
            dma((1,)),
            dma((1,)),
            dma((1,)),
            dma((PIECES,)),
            dma((1,)),
            dma((PIECES // 2,)),
            pltpu.SemaphoreType.REGULAR,
            dma((1,)),
            dma((1,)),
            dma((1,)),
            dma((1,)),
            dma((1,)),
            dma((CUTS, 4)),
            dma((1,)),
            dma((CUTS,)),
            dma((1,)),
            dma((CUTS,)),
            dma((1,)),
            dma((1,)),
        ],
        compiler_params=pltpu.CompilerParams(
            collective_id=0, has_side_effects=True, vmem_limit_bytes=56 * 1024 * 1024
        ),
        cost_estimate=pl.CostEstimate(
            flops=6 * n_rows * width * shard, bytes_accessed=4 * width * shard, transcendentals=0
        ),
        name="divergence_heads",
    )(
        pol_hidden,
        ref_hidden,
        pol_head,
        ref_head,
        kept.reshape(1, per_group),
        send_counts,
        lengths.reshape(1, 2),
    )
    return pl.pallas_call(
        split,
        out_shape=(
            jax.ShapeDtypeStruct((3, n_rows // GROUPS), F32),
            jax.ShapeDtypeStruct((4, width), F32),
        ),
        in_specs=[vmem],
        out_specs=(vmem, vmem),
        name="split_outputs",
    )(both)


def solution(mesh):
    return jax.shard_map(
        body,
        mesh=mesh,
        in_specs=(
            P("dp", None),
            P("dp", None),
            P(None, ("dp", "vocab")),
            P(None, ("dp", "vocab")),
            P("dp"),
            P("dp", None),
            P("dp"),
        ),
        out_specs=(P(None, "dp"), P(("dp", "vocab"), None)),
        check_vma=False,
    )
```

```python
import functools

import jax
import jax.numpy as jnp
from jax import lax
from jax.experimental import pallas as pl
from jax.experimental.pallas import tpu as pltpu
from jax.sharding import PartitionSpec as P

MESH = pl.DeviceIdType.MESH
GROUPS = 8
PEERS = 16
SPAN = 32
PIECES = 8
CUTS = 2
LAG = 3
WIDE = 1
FETCHED = PIECES + 3 * WIDE
POSTED = 6
F32 = jnp.float32
BF16 = jnp.bfloat16


def dot(a, b):
    return lax.dot_general(a, b, (((1,), (0,)), ((), ())), preferred_element_type=F32)


def dot_t(a, b):
    return lax.dot_general(a, b, (((1,), (1,)), ((), ())), preferred_element_type=F32)


def iota(shape, axis):
    return lax.broadcasted_iota(jnp.int32, shape, axis)


def merge_stats(block):
    top_p, top_r = block[:, 0, :], block[:, 1, :]
    s0, s1, s2 = block[:, 2, :], block[:, 3, :], block[:, 4, :]
    r0, r1 = block[:, 5, :], block[:, 6, :]
    best_p = jnp.max(top_p, axis=0, keepdims=True)
    best_r = jnp.max(top_r, axis=0, keepdims=True)
    low_p, low_r = top_p - best_p, top_r - best_r
    shift = low_p - low_r
    scale_p, scale_r = jnp.exp(low_p), jnp.exp(low_r)

    def total(value):
        return jnp.sum(value, axis=0, keepdims=True)

    return (
        best_p,
        best_r,
        total(scale_p * s0),
        total(scale_p * (s1 + shift * s0)),
        total(scale_p * (s2 + shift * (2.0 * s1 + shift * s0))),
        total(scale_r * r0),
        total(scale_r * (r1 + shift * r0)),
    )


def kernel(
    pol_hidden,
    ref_hidden,
    pol_head,
    ref_head,
    kept,
    counts,
    lengths,
    out,
    head,
    gath,
    rows,
    acc,
    logt,
    slope,
    info,
    sel,
    selt,
    length_row,
    stat_v,
    stat_d,
    a_src,
    a_dst,
    own,
    b_src,
    b_dst,
    c_src,
    c_dst,
    d_src,
    d_dst,
    head_sem,
    p1_send,
    p1_recv,
    info_send,
    info_recv,
    ring_send,
    ring_recv,
    sib_send,
    sib_recv,
    token,
    sv_send,
    sv_recv,
    sd_send,
    sd_recv,
    a_send,
    a_recv,
    b_send,
    b_recv,
    c_send,
    c_recv,
    d_send,
    d_recv,
):
    group = lax.axis_index("dp")
    v = lax.axis_index("vocab")
    y, c = group // 2, group % 2
    z, x = v // 4, v % 4
    f = x * (1 - c) + z * c
    s = z * (1 - c) + x * c
    per_group, width = pol_hidden.shape
    part = width // (4 * PIECES)
    half = width // 2
    shard = pol_head.shape[1]
    n_rows = rows.shape[2]

    def vid(df, ds):
        ff, ss = (f + df) % 4, (s + ds) % 4
        return ff * (1 + 3 * c) + ss * (4 - 3 * c)

    def remote(src, dst, send, recv, dp=None, vocab=None):
        target = {}
        if dp is not None:
            target["dp"] = dp
        if vocab is not None:
            target["vocab"] = vocab
        return pltpu.make_async_remote_copy(
            src_ref=src,
            dst_ref=dst,
            send_sem=send,
            recv_sem=recv,
            device_id=target,
            device_id_type=MESH,
        )

    sibling = group + 1 - 2 * c

    def await_in(like, sem):
        remote(like, like, sem, sem, dp=sibling).wait_recv()

    def await_out(like, sem):
        remote(like, like, sem, sem, dp=sibling).wait_send()

    drains = []

    def finish():
        while drains:
            drains.pop(0)()


    quarter = width // 4
    for m, source in enumerate((pol_head, ref_head)):
        for q in range(4):
            at = pl.ds(q * quarter, quarter)
            pltpu.make_async_copy(source.at[at], head.at[m, at], head_sem.at[0]).start()
    barrier = pltpu.get_barrier_semaphore()
    for j in (4, 3, 5, 2, 6, 1, 7):
        pl.semaphore_signal(
            barrier, inc=1, device_id={"dp": (group + j) % GROUPS}, device_id_type=MESH
        )
    for ds in (1, 2, 3):
        pl.semaphore_signal(
            barrier, inc=1, device_id={"vocab": vid(0, ds)}, device_id_type=MESH
        )
    info[group] = jnp.zeros(info.shape[1:], jnp.int32)
    info[group, 0:1, 0:per_group] = kept[...]
    info[group, 1:2, 0:GROUPS] = counts[...]
    info[group, 2:3, 0:2] = lengths[...]
    acc[...] = jnp.zeros(acc.shape, F32)
    pl.semaphore_wait(barrier, GROUPS + 2)

    for j in (4, 3, 5, 2, 6, 1, 7):
        remote(
            info.at[group],
            info.at[group],
            info_send.at[0],
            info_recv.at[0],
            dp=(group + j) % GROUPS,
        ).start()
    hiddens = (pol_hidden, ref_hidden)

    def fetched(q, quarter):
        extra = jnp.maximum(q - PIECES + WIDE, 0)
        piece = jnp.where(q < PIECES - WIDE, q, PIECES - WIDE + extra // 4)
        return (quarter + extra % 4) % 4 * PIECES + piece

    def part_source(m, q):
        at = pl.multiple_of(fetched(q, (z, x)[m]) * part, part)
        return hiddens[m].at[:, pl.ds(at, part)]

    def part_copy(m, dy, q):
        return remote(
            part_source(m, q),
            gath.at[q, group],
            p1_send.at[0],
            p1_recv.at[q],
            dp=2 * ((y + dy) % 4) + m,
        )

    def local_copy(m, q):
        return pltpu.make_async_copy(part_source(m, q), gath.at[q, group], p1_recv.at[q])

    def each_part(q, act):
        for dy in (2, 1, 3):
            for m in (0, 1):
                act(part_copy(m, dy, q))
        for m in (0, 1):

            @pl.when(c != m)
            def _():
                act(part_copy(m, 0, q))

    def start_parts(q):
        each_part(q, lambda copy: copy.start())
        for m in (0, 1):

            @pl.when(c == m)
            def _():
                local_copy(m, q).start()

    for q in range(POSTED):
        start_parts(q)


    def drain_parts():
        await_out(info.at[pl.ds(0, GROUPS - 1)], info_send.at[0])
        for q in range(FETCHED):
            await_out(gath.at[q, pl.ds(0, GROUPS - 1)], p1_send.at[0])

    drains.append(drain_parts)

    await_in(info.at[pl.ds(0, GROUPS - 1)], info_recv.at[0])
    kept_g = jnp.concatenate([info[i, 0:1, :] for i in range(GROUPS)], axis=0).astype(F32)
    count_g = jnp.concatenate([info[i, 1:2, :] for i in range(GROUPS)], axis=0).astype(F32)
    length_g = jnp.concatenate([info[i, 2:3, :] for i in range(GROUPS)], axis=0).astype(F32)
    upper = (iota((128, 128), 0) < iota((128, 128), 1)).astype(F32)
    rank = dot(kept_g, upper)
    start = dot(count_g, upper)
    line = jnp.zeros((1, 128), F32)
    lines = []
    for i in range(GROUPS):
        lines.append(line)
        line = line + count_g[i : i + 1, :]
    offset = jnp.concatenate(lines, axis=0)
    placed = jnp.zeros((GROUPS, 128), F32)
    for j in range(GROUPS):
        first = start[:, j : j + 1]
        last = first + count_g[:, j : j + 1]
        target = float(j * (n_rows // GROUPS)) + offset[:, j : j + 1] + rank - first
        placed = placed + jnp.where((first <= rank) & (rank < last), target, 0.0)
    placed = jnp.where(kept_g > 0.5, placed, -1.0)
    lane = iota((GROUPS, 128), 1)
    length_g = jnp.where(lane < SPAN, length_g[:, 0:1], length_g[:, 1:2])
    length_g = jnp.where(kept_g > 0.5, length_g, 0.0)
    placed_r = pltpu.roll(placed, 64, 1)
    length_r = pltpu.roll(length_g, 64, 1)
    place = iota((n_rows, 128), 0).astype(F32)
    low = lane[0:1] < 64
    weight_len = jnp.zeros((8, n_rows), F32)
    for k in range(4):
        pair = jnp.where(low, placed[2 * k : 2 * k + 1], placed_r[2 * k + 1 : 2 * k + 2])
        spans = jnp.where(low, length_g[2 * k : 2 * k + 1], length_r[2 * k + 1 : 2 * k + 2])
        chosen = (place == pair).astype(F32)
        sel[:, k * 128 : (k + 1) * 128] = chosen.astype(BF16)
        weight_len = weight_len + dot_t(jnp.broadcast_to(spans, (8, 128)), chosen)
    length_row[...] = weight_len

    line = iota((2 * n_rows, 2 * n_rows), 0)
    to_f, to_c, to_s = line // 32 % 4, line // 16 % 2, line // 4 % 4
    to_v = to_f * (1 + 3 * c) + to_s * (4 - 3 * c)
    origin = (line // 128 * 2 + to_c) * per_group + to_v * 4 + line % 4
    moved = (iota((2 * n_rows, 2 * n_rows), 1) == origin).astype(F32).astype(BF16)
    selt[...] = dot_t(moved, sel[...]).astype(BF16)
    pltpu.make_async_copy(head, head, head_sem.at[0]).wait()

    def push(slot, q, j):
        return remote(
            rows.at[c, slot],
            rows.at[c, slot],
            ring_send.at[0],
            ring_recv.at[q],
            vocab=vid(0, (2, 1, 3)[j]),
        )

    def share(model, slot):
        return remote(
            rows.at[model, slot],
            rows.at[model, slot],
            sib_send.at[0],
            sib_recv.at[slot % PIECES // 2],
            dp=sibling,
        )

    def order(j):
        return jnp.where(j == 1, 1, jnp.where(j == 2, 3, jnp.where(j == 3, 2, 0)))

    def multiply(model, first, q):
        total = acc[model]
        for k in range(4):
            slot = ((first + k) % 4) * PIECES + 2 * q
            at = pl.ds(pl.multiple_of(slot * part, 2 * part), 2 * part)
            both = jnp.concatenate([rows[model, slot], rows[model, slot + 1]], axis=1)
            total = total + dot(both, head[model, at, :])
        acc[model] = total

    def parts_step(p, carry):
        @pl.when(p < FETCHED)
        def _():
            await_in(gath.at[p], p1_recv.at[p])
            slot = fetched(p, s)
            packed = gath[p].reshape(GROUPS * per_group, part)
            rows[c, slot] = dot(sel[...], packed).astype(BF16)

            @pl.when(p < PIECES - WIDE)
            def _():
                for j in range(3):
                    push(slot, p, j).start()

            share(c, slot).start()

            @pl.when(p < FETCHED - POSTED)
            def _():
                start_parts(p + POSTED)


        def side(i, carry):
            t = p - LAG - 1 + i
            mine = i == 1
            first = jnp.where(mine, s, f)
            model = jnp.where(mine, c, 1 - c)

            @pl.when((t >= 0) & (t < PIECES))
            def _():
                @pl.when(mine & (t < PIECES - WIDE))
                def _():
                    await_in(rows.at[c, pl.ds(0, 3)], ring_recv.at[t])
                    for j in range(3):
                        share(c, (s + 1 + j) % 4 * PIECES + t).start()

                @pl.when(t % 2 == 1)
                def _():
                    @pl.when(i == 0)
                    def _():
                        await_in(rows.at[1 - c, pl.ds(0, 8)], sib_recv.at[t // 2])

                    multiply(model, first, t // 2)

            return carry

        lax.fori_loop(0, 2, side, 0)
        return carry

    lax.fori_loop(0, PIECES + LAG + 1, parts_step, 0)

    def drain_ring():
        await_out(rows.at[0, pl.ds(0, 3 * (PIECES - WIDE))], ring_send.at[0])
        await_out(rows.at[0], sib_send.at[0])

    drains.append(drain_ring)

    chunks = shard // 128
    for m in (0, 1):
        for q in range(chunks):
            at = slice(q * 128, (q + 1) * 128)
            logt[m, at, :] = jnp.transpose(acc[m, :, at])
    top_p = jnp.max(logt[0], axis=0, keepdims=True)
    top_r = jnp.max(logt[1], axis=0, keepdims=True)
    step = 64
    zero = jnp.zeros((8, n_rows), F32)

    def fold(value):
        return jnp.sum(value.reshape(step // 8, 8, n_rows), axis=0)

    def local_sums(q, carry):
        s0, s1, s2, r0, r1 = carry
        at = pl.ds(pl.multiple_of(q * step, step), step)
        lp = logt[0, at, :] - top_p
        lr = logt[1, at, :] - top_r
        ep, er = jnp.exp(lp), jnp.exp(lr)
        d = lp - lr
        ed = ep * d
        return (
            s0 + fold(ep),
            s1 + fold(ed),
            s2 + fold(ed * d),
            r0 + fold(er),
            r1 + fold(er * d),
        )

    sums = lax.fori_loop(0, shard // step, local_sums, (zero,) * 5)
    sums = [jnp.sum(value, axis=0, keepdims=True) for value in sums]
    blank = jnp.zeros((1, n_rows), F32)
    stat_d[group] = jnp.concatenate([top_p, top_r, *sums, blank], axis=0)
    for j in (4, 3, 5, 2, 6, 1, 7):
        remote(
            stat_d.at[group],
            stat_d.at[group],
            sd_send.at[0],
            sd_recv.at[0],
            dp=(group + j) % GROUPS,
        ).start()
    for ds in (1, 2, 3):
        pl.semaphore_signal(token, inc=1, device_id={"vocab": vid(0, ds)}, device_id_type=MESH)
    await_in(stat_d.at[pl.ds(0, GROUPS - 1)], sd_recv.at[0])
    pl.semaphore_wait(token, 3)

    def drain_stat_d():
        await_out(stat_d.at[pl.ds(0, GROUPS - 1)], sd_send.at[0])

    drains.append(drain_stat_d)
    stat_v[v] = jnp.concatenate([*merge_stats(stat_d), blank], axis=0)
    for j in (10, 6, 9, 11, 14, 2, 8, 5, 7, 13, 15, 1, 3, 4, 12):
        remote(
            stat_v.at[v], stat_v.at[v], sv_send.at[0], sv_recv.at[0], vocab=(v + j) % PEERS
        ).start()
    finish()
    await_in(stat_v.at[pl.ds(0, PEERS - 1)], sv_recv.at[0])

    def drain_stat_v():
        await_out(stat_v.at[pl.ds(0, PEERS - 1)], sv_send.at[0])

    drains.append(drain_stat_v)
    top_p, top_r, s0, s1, s2, r0, r1 = merge_stats(stat_v)
    log_s, log_r = jnp.log(s0), jnp.log(r0)
    norm_p, norm_r = top_p + log_s, top_r + log_r
    move = log_r - log_s
    forward = s1 / s0 + move
    squared = 0.5 * ((s2 + move * (2.0 * s1)) / s0 + move * move)
    reverse = -(r1 / r0 + move)
    both = forward + squared
    weight = float(SPAN) / length_row[0:1, :]

    def slopes(q, carry):
        at = pl.ds(pl.multiple_of(q * step, step), step)
        lp = logt[0, at, :] - norm_p
        d = lp - (logt[1, at, :] - norm_r)
        slope[at, :] = (weight * jnp.exp(lp) * (0.5 * d * d + d - both)).astype(BF16)
        return carry

    lax.fori_loop(0, shard // step, slopes, 0)

    chunk = half // 4
    order_s = (2, 1, 3, 0)

    cut = chunk // CUTS

    def start_of(core, index, h):
        return pl.multiple_of(core * half + index * chunk + h * cut, cut)

    def a_copy(h, t):
        return remote(
            a_src.at[h, t], a_dst.at[h, t], a_send.at[0], a_recv.at[h, t], dp=sibling
        )

    def b_copy(h, t):
        return remote(
            b_src.at[h, t],
            b_dst.at[h, t],
            b_send.at[0],
            b_recv.at[h],
            vocab=vid(0, order_s[t]),
        )

    def gradient(h, carry):
        def theirs(t):
            at = start_of(1 - c, (f + order_s[t]) % 4, h)
            a_src[h, t] = dot(head[0, pl.ds(at, cut), :], slope[...]).astype(BF16)
            a_copy(h, t).start()

        def mine(t):
            at = start_of(c, (s + order_s[t]) % 4, h)
            own[h] = dot(head[0, pl.ds(at, cut), :], slope[...])

        theirs(0)
        theirs(1)
        for t in range(3):
            mine(t)
            if t < 2:
                theirs(t + 2)
            a_copy(h, t).wait_recv()
            b_src[h, t] = (own[h] + a_dst[h, t].astype(F32)).astype(BF16)
            b_copy(h, t).start()
        mine(3)
        a_copy(h, 3).wait_recv()
        own[h] = own[h] + a_dst[h, 3].astype(F32)
        return carry

    lax.fori_loop(0, CUTS, gradient, 0)

    def drain_b():
        for h in range(CUTS):
            await_out(a_src.at[h], a_send.at[0])
            await_out(b_src.at[h], b_send.at[0])

    drains.append(drain_b)

    here = y * 4 + f

    def c_copy(h, j):
        to_y, to_f = (y + j // 4) % 4, (f + j % 4) % 4
        other = to_y * 4 + to_f
        return remote(
            c_src.at[h, other],
            c_dst.at[h, here],
            c_send.at[0],
            c_recv.at[h],
            dp=2 * to_y + c,
            vocab=vid(j % 4, 0),
        )

    order_c = (10, 9, 11, 8, 6, 14, 5, 7, 13, 15, 4, 12, 2, 1, 3)
    for h in range(CUTS):
        total = own[h]
        await_in(b_dst.at[h], b_recv.at[h])
        for t in range(3):
            total = total + b_dst[h, t].astype(F32)
        spread = dot_t(selt[...], total.astype(BF16)).astype(BF16)
        c_src[h] = spread.reshape(PEERS, 32, cut)
        for j in order_c:
            c_copy(h, j).start()

    finish()
    stacked = jnp.concatenate([forward, squared, reverse], axis=0)
    share_rows = n_rows // GROUPS
    result = jnp.zeros((3, share_rows), F32)
    for j in range(GROUPS):
        result = jnp.where(group == j, stacked[:, j * share_rows : (j + 1) * share_rows], result)
    out[4:7, 0:share_rows] = result

    for h in range(CUTS):
        c_dst[h, here] = c_src[h, here]
        await_in(c_dst.at[h, pl.ds(0, PEERS - 1)], c_recv.at[h])
        value = c_dst[h, 0].astype(F32)
        for k in range(1, PEERS):
            value = value + c_dst[h, k].astype(F32)
        d_src[:, h * cut : (h + 1) * cut] = value

    def drain_c():
        for h in range(CUTS):
            await_out(c_src.at[h, pl.ds(0, PEERS - 1)], c_send.at[0])

    drains.append(drain_c)

    def d_copy(dc, ds):
        to_c, to_s = (c + dc) % 2, (s + ds) % 4
        at = pl.multiple_of(to_c * 16 + to_s // 2 * 8, 8)
        return remote(
            d_src.at[pl.ds(at, 8)],
            d_dst.at[c * 4 + s],
            d_send.at[0],
            d_recv.at[0],
            dp=2 * y + to_c,
            vocab=vid(0, ds),
        )

    others = [(dc, ds) for ds in (2, 1, 3, 0) for dc in (0, 1) if (dc, ds) != (0, 0)]
    for dc, ds in others:
        d_copy(dc, ds).start()
    finish()
    d_dst[c * 4 + s] = d_src[pl.ds(pl.multiple_of(c * 16 + s // 2 * 8, 8), 8), :]
    await_in(d_dst.at[pl.ds(0, GROUPS - 1)], d_recv.at[0])
    for u in range(GROUPS):
        odd = (z, x)[u // 4] % 2 == 1
        out[0:4, u * chunk : (u + 1) * chunk] = jnp.where(
            odd, d_dst[u, 4:8, :], d_dst[u, 0:4, :]
        )

    def drain_d():
        await_out(d_dst.at[pl.ds(0, GROUPS - 1)], d_send.at[0])

    drains.append(drain_d)
    finish()


def split(both, div_out, grad_out):
    div_out[...] = both[4:7, 0 : div_out.shape[1]]
    grad_out[...] = both[0:4, :]


def body(pol_hidden, ref_hidden, pol_head, ref_head, kept, send_counts, lengths):
    per_group, width = pol_hidden.shape
    shard = pol_head.shape[1]
    n_rows = GROUPS * per_group // 2
    part = width // (4 * PIECES)
    chunk = width // 8
    cut = chunk // CUTS
    vmem = pl.BlockSpec(memory_space=pltpu.VMEM)
    hbm = pl.BlockSpec(memory_space=pl.ANY)
    dma = pltpu.SemaphoreType.DMA
    both = pl.pallas_call(
        kernel,
        out_shape=jax.ShapeDtypeStruct((8, width), F32),
        in_specs=[hbm, hbm, hbm, hbm, vmem, vmem, vmem],
        out_specs=vmem,
        scratch_shapes=[
            pltpu.VMEM((2, width, shard), BF16),
            pltpu.VMEM((FETCHED, GROUPS, per_group, part), BF16),
            pltpu.VMEM((2, 4 * PIECES, n_rows, part), BF16),
            pltpu.VMEM((2, n_rows, shard), F32),
            pltpu.VMEM((2, shard, n_rows), F32),
            pltpu.VMEM((shard, n_rows), BF16),
            pltpu.VMEM((GROUPS, 8, 128), jnp.int32),
            pltpu.VMEM((n_rows, 2 * n_rows), BF16),
            pltpu.VMEM((2 * n_rows, n_rows), BF16),
            pltpu.VMEM((8, n_rows), F32),
            pltpu.VMEM((PEERS, 8, n_rows), F32),
            pltpu.VMEM((GROUPS, 8, n_rows), F32),
            pltpu.VMEM((CUTS, 4, cut, n_rows), BF16),
            pltpu.VMEM((CUTS, 4, cut, n_rows), BF16),
            pltpu.VMEM((CUTS, cut, n_rows), F32),
            pltpu.VMEM((CUTS, 3, cut, n_rows), BF16),
            pltpu.VMEM((CUTS, 3, cut, n_rows), BF16),
            pltpu.VMEM((CUTS, PEERS, 32, cut), BF16),
            pltpu.VMEM((CUTS, PEERS, 32, cut), BF16),
            pltpu.VMEM((32, chunk), F32),
            pltpu.VMEM((GROUPS, 8, chunk), F32),
            dma((1,)),
            dma((1,)),
            dma((FETCHED,)),
            dma((1,)),
            dma((1,)),
            dma((1,)),
            dma((PIECES,)),
            dma((1,)),
            dma((PIECES // 2,)),
            pltpu.SemaphoreType.REGULAR,
            dma((1,)),
            dma((1,)),
            dma((1,)),
            dma((1,)),
            dma((1,)),
            dma((CUTS, 4)),
            dma((1,)),
            dma((CUTS,)),
            dma((1,)),
            dma((CUTS,)),
            dma((1,)),
            dma((1,)),
        ],
        compiler_params=pltpu.CompilerParams(
            collective_id=0, has_side_effects=True, vmem_limit_bytes=56 * 1024 * 1024
        ),
        cost_estimate=pl.CostEstimate(
            flops=6 * n_rows * width * shard, bytes_accessed=4 * width * shard, transcendentals=0
        ),
        name="divergence_heads",
    )(
        pol_hidden,
        ref_hidden,
        pol_head,
        ref_head,
        kept.reshape(1, per_group),
        send_counts,
        lengths.reshape(1, 2),
    )
    return pl.pallas_call(
        split,
        out_shape=(
            jax.ShapeDtypeStruct((3, n_rows // GROUPS), F32),
            jax.ShapeDtypeStruct((4, width), F32),
        ),
        in_specs=[vmem],
        out_specs=(vmem, vmem),
        name="split_outputs",
    )(both)


def solution(mesh):
    return jax.shard_map(
        body,
        mesh=mesh,
        in_specs=(
            P("dp", None),
            P("dp", None),
            P(None, ("dp", "vocab")),
            P(None, ("dp", "vocab")),
            P("dp"),
            P("dp", None),
            P("dp"),
        ),
        out_specs=(P(None, "dp"), P(("dp", "vocab"), None)),
        check_vma=False,
    )
```
